256 devices in a mesh: clu: 32 (over x, y, core), blk: 8 (over z).
Axes of the slice: x: 4, y: 4, z: 8, core: 2. Of those that a mesh axis runs over, the one named last changes fastest.
Arguments:
- embeddings: float32 [131072, 768], P(('clu', 'blk')), may hold values from -6 to 6
- cluster_ids: int32 [131072, 1], P(('clu', 'blk')), may hold values from 0 to 31; in each aligned block of 512 rows (0 to 511, 512 to 1023, ...) at most 32 rows name the same one
- ranks: int32 [131072], P(('clu', 'blk')), may hold values from 0 to 1048575
Outputs:
- nearest: float32 [131072], P(('clu', 'blk'))
The draws below stay inside these ranges and needn't reach their ends.
Inputs may be any that keep to these rules, and one draw needn't show every extreme that they name: `cluster_ids`: at most 32 of the rows held by one device name the same cluster, and in every draw some device's rows name one cluster exactly 32 times.
All inputs are finite; a program needn't handle non-finite values.
Results may differ from the reference program's by a relative error of at most 0.0012.
Values may be sent and summed in bfloat16 or wider, within the bound.
No kernel may reach another device: no remote copies, remote signals or barrier semaphores. Data moves between devices by JAX's collectives and lax.ppermute only.
A program may use at most 64 MiB of HBM per device.

```python
import math
import jax
import jax.numpy as jnp
import numpy as np
from jax import lax

D = 768
ROWS_DEV = 512
CAPACITY = 32
ROWS = 131072
N_CLU = 32
N_BLK = 8


def set_ends(entries, key, low, largest):
    place = [jax.random.randint(jax.random.fold_in(key, axis), (), 0, length) for axis, length in enumerate(entries.shape)]
    main_axis = entries.shape.index(max(entries.shape))
    beside = place[:main_axis] + [(place[main_axis] + 1) % entries.shape[main_axis]] + place[main_axis + 1:]
    return entries.at[tuple(place)].set(low).at[tuple(beside)].set(largest)


def block_levels(stream_key, extent, cuts, least, top_value):
    loudness, own = 1.0, jax.random.fold_in(stream_key, 6)
    for axis_at, blocks in cuts:
        draws = jnp.exp(jax.random.uniform(jax.random.fold_in(own, axis_at), (blocks,), jnp.float32, least / len(cuts), top_value / len(cuts)))
        loudness = loudness * jnp.repeat(draws, extent[axis_at] // blocks).reshape([-1 if axis == axis_at else 1 for axis in range(len(extent))])
    return loudness


def routed_block(rng, own, number, rows, number_of, top, bound, slope):
    sequence = jax.random.permutation(rng, number_of)
    packed, ordinary = portions_of(number_of, rows * top, bound, slope, True), portions_of(number_of, rows * top, bound, slope, False)
    places = jnp.arange(number_of)

    def named(sizes, rotation):
        used = int((sizes > 0).sum())
        fixed = max(1, used // 4)
        passed = fixed + (places - fixed + rotation * (used - fixed)) % max(1, number_of - fixed)
        return jnp.zeros((number_of,), jnp.int32).at[sequence[jnp.where(places < fixed, places, passed)]].set(jnp.asarray(sizes, jnp.int32))

    sizes = jnp.where(number % 4 == 0, named(packed, number // 4), named(ordinary, number - number // 4 - 1))
    mixed = jax.random.permutation(jax.random.fold_in(own, 3), number_of)
    donor, receiver = mixed[0:number_of // 2 * 2:2], mixed[1:number_of // 2 * 2:2]
    margin = jnp.minimum(sizes[donor] - 1, bound - sizes[receiver]) // 2
    margin = jnp.where((donor == sequence[0]) | (receiver == sequence[0]) | (sizes[receiver] == 0), 0, jnp.maximum(margin, 0))
    passed = jax.random.randint(jax.random.fold_in(own, 4), (number_of // 2,), 0, 1 << 20) % (margin + 1)
    sizes = sizes.at[donor].add(-passed).at[receiver].add(passed)
    members = jnp.searchsorted(jnp.cumsum(sizes), jnp.arange(rows * top), side="right").astype(jnp.int32)
    listing = members.reshape(top, rows).T
    listing = listing[jax.random.permutation(jax.random.fold_in(own, 1), rows)]
    rotation = jax.random.randint(jax.random.fold_in(own, 2), (rows, 1), 0, top)
    return jnp.take_along_axis(listing, (jnp.arange(top)[None, :] + rotation) % top, axis=1)


def portions_of(amount, total, most, lean, full):
    weights = [(1 << 20) // math.isqrt(rank ** lean) + 1 for rank in range(1, amount + 1)]
    largest = most if full else min(most, max(-(-total // amount), total * weights[0] // sum(weights)))
    least = 1 if total - largest >= amount - 1 else 0
    given, surplus = [largest] + [least] * (amount - 1), total - largest - least * (amount - 1)
    while surplus > 0:
        movable = [i for i in range(1, amount) if given[i] < largest] or [i for i in range(1, amount) if given[i] < most]
        whole, left = sum([weights[i] for i in movable]), surplus
        for i in movable:
            extra = min(most - given[i], max(1, left * weights[i] // whole), surplus)
            given[i] = given[i] + extra
            surplus = surplus - extra
    return np.array(given)


def normal_values(own_key, dims, spread, bound, shards=(), held_as=jnp.bfloat16):
    factor_of = block_levels(own_key, dims, shards, -0.22, 0.18) if shards else 1.0
    drawn = jax.random.normal(own_key, dims, jnp.float32) * spread * factor_of
    return jnp.minimum(jnp.maximum(drawn, -bound), bound).astype(held_as)


def setup_inputs(seed: int = 0) -> dict:
    arg_keys = jax.random.split(jax.random.key(seed), 4)
    embeddings = normal_values(arg_keys[0], (ROWS, D), 1.0, 6.0, ((0, 256),), jnp.float32)
    cluster_ids_keys = jax.random.split(jax.random.fold_in(arg_keys[1], 1), ROWS // ROWS_DEV)
    cluster_ids_turns = jax.random.permutation(jax.random.fold_in(arg_keys[1], 3), ROWS // ROWS_DEV)
    cluster_ids = jax.vmap(lambda own, number: routed_block(jax.random.fold_in(arg_keys[1], 2), own, number, ROWS_DEV, N_CLU, 1, CAPACITY, 2))(cluster_ids_keys, cluster_ids_turns).reshape((ROWS, 1))
    ranks = set_ends(jax.random.randint(arg_keys[2], (ROWS,), 0, 8 * ROWS), jax.random.fold_in(arg_keys[2], 1), 0, (8 * ROWS) - 1).astype(jnp.int32)
    return dict(embeddings=embeddings, cluster_ids=cluster_ids, ranks=ranks)


def normalize_rows(rows):
    norms = lax.optimization_barrier(jnp.sum(rows * rows, axis=1, keepdims=True))
    return (rows * lax.rsqrt(norms + 1e-06)).astype(jnp.bfloat16)

def reference(embeddings, cluster_ids, ranks):
    unit = normalize_rows(embeddings)
    ident = cluster_ids[:, 0].astype(jnp.int32)
    total = ident.shape[0]
    window = N_CLU * N_BLK * CAPACITY
    block_rows = math.gcd(window, 512)
    order = jnp.argsort(ident, stable=True).astype(jnp.int32)
    sorted_unit = jnp.concatenate([unit[order].astype(jnp.float32), jnp.zeros((window, D), jnp.float32)], axis=0)
    sorted_rank = jnp.concatenate([ranks[order].astype(jnp.int32), jnp.full((window,), -1, jnp.int32)])
    sorted_ident = jnp.concatenate([ident[order], jnp.full((window,), -1, jnp.int32)])
    counts = lax.optimization_barrier(jnp.sum((ident[:, None] == jnp.arange(N_CLU, dtype=jnp.int32)[None, :]).astype(jnp.int32), axis=0)).astype(jnp.int32)
    starts = (jnp.cumsum(counts) - counts).astype(jnp.int32)

    def one_cluster(result, cluster):
        begin = starts[cluster].astype(jnp.int32)
        keys = lax.dynamic_slice_in_dim(sorted_unit, begin, window, 0)
        key_rank = lax.dynamic_slice_in_dim(sorted_rank, begin, window, 0)
        member = lax.dynamic_slice_in_dim(sorted_ident, begin, window, 0) == cluster
        query_blocks = keys.reshape(window // block_rows, block_rows, D)
        rank_blocks = key_rank.reshape(window // block_rows, block_rows)

        def one_block(item):
            queries, query_rank = item
            scores = jnp.dot(queries, keys.T, precision=lax.Precision.HIGHEST)
            allowed = member[None, :] & (key_rank[None, :] < query_rank[:, None])
            return lax.optimization_barrier(jnp.max(jnp.where(allowed, scores, -1.0), axis=1))
        values = lax.map(one_block, (query_blocks, rank_blocks)).reshape(window)
        current = lax.dynamic_slice_in_dim(result, begin, window, 0)
        updated = jnp.where(member, values, current)
        return (lax.dynamic_update_slice_in_dim(result, updated, begin, 0), None)
    initial = jnp.full((total + window,), -1.0, jnp.float32)
    result, _ = lax.scan(one_cluster, initial, jnp.arange(N_CLU, dtype=jnp.int32))
    return jnp.zeros((total,), jnp.float32).at[order].set(result[:total])
```

```python
import functools

import jax
import jax.numpy as jnp
from jax import lax
from jax.experimental import pallas as pl
from jax.experimental.pallas import tpu as pltpu
from jax.sharding import Mesh, PartitionSpec as P

D = 768
ROWS = 512
GROUPS = 32
HALF = 16
PARTS = D // 128
SIZE = {"x": 4, "y": 4, "c": 2, "z": 8}
LIMIT = 60 * 1024 * 1024
NT = (((1,), (1,)), ((), ()))
NN = (((1,), (0,)), ((), ()))


def dot(a, b, dims):
    return lax.dot_general(a, b, dims, preferred_element_type=jnp.float32)


def to_lanes(column):
    return jnp.broadcast_to(column, (column.shape[0], 128)).T[0:1, :]


def pack_kernel(emb_ref, ids_ref, rank_ref, first_ref, second_ref, pos_ref):
    rows = emb_ref[...]
    norms = jnp.sum(rows * rows, axis=1, keepdims=True)
    unit = (rows * lax.rsqrt(norms + 1e-06)).astype(jnp.bfloat16)

    lane = lax.broadcasted_iota(jnp.int32, (ROWS, 128), 1)
    target = ids_ref[...]
    member = (target == lane).astype(jnp.float32)
    earlier = lax.broadcasted_iota(jnp.int32, (ROWS, ROWS), 1) < lax.broadcasted_iota(
        jnp.int32, (ROWS, ROWS), 0
    )
    before = dot(earlier.astype(jnp.bfloat16), member.astype(jnp.bfloat16), NN)
    slot = jnp.sum(before * member, axis=1, keepdims=True).astype(jnp.int32)
    position = (slot // HALF) * (GROUPS * HALF) + target * HALF + slot % HALF
    pos_ref[...] = position

    at = to_lanes(position.astype(jnp.float32)).astype(jnp.int32)
    rank = rank_ref[...]
    high, mid, low = (rank >> 14) - 128, (rank >> 7) & 127, rank & 127

    def rank_lanes(start):
        parts = jnp.where(lane == start, high, 0)
        parts = jnp.where(lane == start + 1, mid, parts)
        return jnp.where(lane == start + 2, low, parts).astype(jnp.float32).astype(jnp.bfloat16)

    def pick(half):
        slots = lax.broadcasted_iota(jnp.int32, (GROUPS * HALF, ROWS), 0) + half * GROUPS * HALF
        return (slots == at).astype(jnp.float32).astype(jnp.bfloat16)

    ranks = jnp.zeros((GROUPS * HALF, 128), jnp.float32)
    for half, out_ref in enumerate((first_ref, second_ref)):
        chosen = pick(half)
        moved = dot(chosen, unit, NN).astype(jnp.bfloat16)
        for part in range(PARTS):
            out_ref[:, part * HALF : (part + 1) * HALF, :] = moved[
                :, part * 128 : (part + 1) * 128
            ].reshape(GROUPS, HALF, 128)
        ranks += dot(chosen, rank_lanes(3 * half), NN)
    first_ref[:, D // 8 :, :] = ranks.astype(jnp.bfloat16).reshape(GROUPS, HALF, 128)


def vmem(count):
    return [pl.BlockSpec(memory_space=pltpu.VMEM)] * count


def pack(embeddings, ids, ranks):
    return pl.pallas_call(
        pack_kernel,
        out_shape=(
            jax.ShapeDtypeStruct((GROUPS, D // 8 + HALF, 128), jnp.bfloat16),
            jax.ShapeDtypeStruct((GROUPS, D // 8, 128), jnp.bfloat16),
            jax.ShapeDtypeStruct((ROWS, 1), jnp.int32),
        ),
        in_specs=vmem(3),
        out_specs=tuple(vmem(3)),
        compiler_params=pltpu.CompilerParams(vmem_limit_bytes=LIMIT),
        name="pack",
    )(embeddings, ids, ranks)


def keys_of(ref):
    wide = [
        ref[:, part * HALF : (part + 1) * HALF, :].reshape(GROUPS * HALF, 128)
        for part in range(PARTS)
    ]
    return jnp.concatenate(wide, axis=1)


def rank_weights(shape, axis, start):
    place = lax.broadcasted_iota(jnp.int32, shape, axis) - start
    weights = jnp.where(place == 0, 16384.0, jnp.where(place == 1, 128.0, 1.0))
    return jnp.where((place >= 0) & (place < 3), weights, 0.0).astype(jnp.bfloat16)


def score_kernel(names, pairs, finals, *refs):
    firsts = sorted({name[0] for name in names})
    data = dict(zip(names, refs))
    carried = refs[len(names)]
    out_ref = refs[len(names) + 1]
    keys = {name: keys_of(data[name]) for name in names}
    by_row, by_lane = {}, {}
    for block in firsts:
        tile = data[block + "0"][:, D // 8 :, :].reshape(GROUPS * HALF, 128)
        for half in range(2):
            name = block + str(half)
            if name in names:
                by_row[name] = dot(tile, rank_weights((128, 128), 0, 3 * half), NN)
                by_lane[name] = dot(rank_weights((8, 128), 1, 3 * half), tile, NT)[0:1]
    best_row, best_lane = {}, {}
    for rows, columns, forward, backward in pairs:
        scores = dot(keys[rows], keys[columns], NT)
        row_rank = jnp.concatenate([by_row[rows]] * 4, axis=1)
        lane_rank = by_lane[columns]
        if forward:
            kept = jnp.where(lane_rank < row_rank, scores, -1.0)
            folded = functools.reduce(
                jnp.maximum, [kept[:, 128 * i : 128 * (i + 1)] for i in range(4)]
            )
            best_row[rows] = jnp.maximum(best_row[rows], folded) if rows in best_row else folded
        if backward:
            kept = jnp.where(row_rank < lane_rank, scores, -1.0)
            folded = jnp.max(kept, axis=0, keepdims=True)
            if columns in best_lane:
                folded = jnp.maximum(best_lane[columns], folded)
            best_lane[columns] = folded
    for index, name in enumerate(finals):
        value = carried[index : index + 1, :]
        if name in best_lane:
            value = jnp.maximum(value, best_lane[name])
        if name in best_row:
            value = jnp.maximum(value, jnp.max(best_row[name].T, axis=0, keepdims=True))
        out_ref[index : index + 1, :] = value


FINALS = ("o0", "o1", "s0", "s1", "b0", "b1", "z0", "z1")


def score(blocks, pairs, carried):
    names = tuple(sorted(blocks))
    return pl.pallas_call(
        functools.partial(score_kernel, names, pairs, FINALS),
        out_shape=jax.ShapeDtypeStruct((8, GROUPS * HALF), jnp.float32),
        in_specs=vmem(len(names) + 1),
        out_specs=vmem(1)[0],
        compiler_params=pltpu.CompilerParams(vmem_limit_bytes=LIMIT),
        cost_estimate=pl.CostEstimate(
            flops=2 * len(pairs) * 512 * 512 * D, bytes_accessed=800000 * len(names), transcendentals=0
        ),
        name="score" + str(len(pairs)),
    )(*[blocks[name] for name in names], carried)


FIRST = (
    ("o0", "o0", True, False),
    ("o0", "s0", True, False),
    ("o0", "b0", True, True),
    ("s0", "b0", True, True),
    ("z0", "b0", True, True),
)
SECOND = (
    ("o1", "o1", True, False),
    ("o0", "o1", True, True),
    ("o1", "s1", True, False),
    ("o0", "s1", True, True),
    ("o0", "b1", True, True),
    ("o1", "b0", True, True),
    ("o1", "b1", True, True),
    ("s0", "b1", True, True),
    ("s1", "b0", True, True),
    ("s1", "b1", True, True),
    ("z0", "b1", True, True),
    ("z1", "b0", True, True),
    ("z1", "b1", True, True),
)

FROM_NEXT = [
    (((x + 1) % 4) * 2 + (c if x < 2 else 1 - c), x * 2 + c) for x in range(4) for c in range(2)
]
FROM_LAST = [(((x - 1) % 4) * 2 + c, x * 2 + c) for x in range(4) for c in range(2)]
SWAP = [(x * 2 + 1 - c, x * 2 + c) for x in range(4) for c in range(2)]


def back(pairs):
    return [(there, here) for here, there in pairs]


def send(array, pairs):
    return lax.ppermute(array, ("x", "c"), pairs)


def spread(part):
    return send(part, SWAP), send(part, FROM_NEXT), send(part, FROM_LAST)


def to_home(array):
    return lax.all_to_all(array, ("y", "z"), split_axis=0, concat_axis=0, tiled=True)


def on_device(embeddings, cluster_ids, ranks):
    first, second, position = pack(embeddings, cluster_ids, ranks.reshape(ROWS, 1))
    o0 = to_home(first)
    s0, b0, z0 = spread(o0)
    o1 = to_home(second)
    s1, b1, z1 = spread(o1)
    best = jnp.full((8, GROUPS * HALF), -1.0, jnp.float32)
    best = score(dict(o0=o0, s0=s0, b0=b0, z0=z0), FIRST, best)
    best = score(dict(o0=o0, s0=s0, b0=b0, z0=z0, o1=o1, s1=s1, b1=b1, z1=z1), SECOND, best)
    own = functools.reduce(
        jnp.maximum,
        [
            best[0:2],
            send(best[2:4], back(SWAP)),
            send(best[4:6], back(FROM_NEXT)),
            send(best[6:8], back(FROM_LAST)),
        ],
    )
    own = own.reshape(2, GROUPS, HALF).transpose(1, 0, 2).reshape(GROUPS, 2 * HALF)
    home = to_home(own).reshape(GROUPS, 2, HALF).transpose(1, 0, 2).reshape(2 * GROUPS * HALF)
    return home[position[:, 0]]


def solution(mesh):
    fine = Mesh(mesh.devices.reshape(tuple(SIZE.values())), tuple(SIZE))
    rows = P(tuple(SIZE))
    return jax.shard_map(
        on_device,
        mesh=fine,
        in_specs=(P(tuple(SIZE), None), P(tuple(SIZE), None), rows),
        out_specs=rows,
        check_vma=False,
    )
```

```python
import functools

import jax
import jax.numpy as jnp
from jax import lax
from jax.experimental import pallas as pl
from jax.experimental.pallas import tpu as pltpu
from jax.sharding import Mesh, PartitionSpec as P

D = 768
ROWS = 512
GROUPS = 32
HALF = 16
SLOTS = 2 * HALF
PART = GROUPS * HALF
PARTS = D // 128
SIZE = {"x": 4, "y": 4, "c": 2, "z": 8}
LIMIT = 60 * 1024 * 1024
NT = (((1,), (1,)), ((), ()))
NN = (((1,), (0,)), ((), ()))
TN = (((0,), (0,)), ((), ()))
BLOCKS = ("o", "s", "b", "z")
FINALS = tuple(block + half for block in BLOCKS for half in "01")


def dot(a, b, dims):
    return lax.dot_general(a, b, dims, preferred_element_type=jnp.float32)


def iota(shape, axis):
    return lax.broadcasted_iota(jnp.int32, shape, axis)


def bits(mask):
    return mask.astype(jnp.float32).astype(jnp.bfloat16)


def three_parts(value):
    parts = []
    for _ in range(3):
        part = value.astype(jnp.bfloat16)
        parts.append(part)
        value = value - part.astype(jnp.float32)
    return parts


def place_rows(unit, slot_at, half, out_ref):
    slot, at = slot_at & (SLOTS - 1), slot_at // SLOTS
    row = jnp.where(slot // HALF == half, at * HALF + slot % HALF, -1)
    chosen = bits(iota((PART, ROWS), 0) == row)
    moved = dot(chosen, unit, NN).astype(jnp.bfloat16)
    for part in range(PARTS):
        out_ref[:, part * HALF : (part + 1) * HALF, :] = moved[
            :, part * 128 : (part + 1) * 128
        ].reshape(GROUPS, HALF, 128)
    return chosen


def pack_first(emb_ref, ids_ref, rank_ref, out_ref, unit_ref, pos_ref):
    rows = emb_ref[...]
    norms = jnp.sum(rows * rows, axis=1, keepdims=True)
    unit = (rows * lax.rsqrt(norms + 1e-06)).astype(jnp.bfloat16)
    unit_ref[...] = unit

    target = ids_ref[...]
    member = (iota((GROUPS, ROWS), 0) == target).astype(jnp.float32)
    earlier = bits(iota((ROWS, ROWS), 0) < iota((ROWS, ROWS), 1))
    before = dot(member.astype(jnp.bfloat16), earlier, NN)
    slot = jnp.sum(before * member, axis=0, keepdims=True).astype(jnp.int32)
    position = target * SLOTS + slot
    pos_ref[...] = position

    first = place_rows(unit, position, 0, out_ref)
    second = bits(
        iota((PART, ROWS), 0) == jnp.where(slot >= HALF, target * HALF + slot - HALF, -1)
    )
    rank = rank_ref[...]
    line = iota((128, ROWS), 0)
    ranks = jnp.zeros((PART, 128), jnp.float32)
    for half, chosen in enumerate((first, second)):
        parts = jnp.zeros((128, ROWS), jnp.int32)
        for index, part in enumerate(((rank >> 14) - 128, (rank >> 7) & 127, rank & 127)):
            parts = jnp.where(line == 3 * half + index, part, parts)
        ranks += dot(chosen, parts.astype(jnp.float32).astype(jnp.bfloat16), NT)
    out_ref[:, D // 8 :, :] = ranks.astype(jnp.bfloat16).reshape(GROUPS, HALF, 128)


def pack_second(unit_ref, pos_ref, out_ref):
    place_rows(unit_ref[...], pos_ref[...], 1, out_ref)


def vmem(count):
    return [pl.BlockSpec(memory_space=pltpu.VMEM)] * count


def call(kernel, name, shapes, *operands, flops=0):
    shapes = tuple(jax.ShapeDtypeStruct(shape, dtype) for shape, dtype in shapes)
    out = pl.pallas_call(
        kernel,
        out_shape=shapes,
        in_specs=vmem(len(operands)),
        out_specs=tuple(vmem(len(shapes))),
        compiler_params=pltpu.CompilerParams(vmem_limit_bytes=LIMIT),
        cost_estimate=pl.CostEstimate(
            flops=flops,
            bytes_accessed=sum(array.size * array.dtype.itemsize for array in operands),
            transcendentals=0,
        ),
        name=name,
    )(*operands)
    return out[0] if len(shapes) == 1 else out


def keys_of(ref):
    wide = [
        ref[:, part * HALF : (part + 1) * HALF, :].reshape(PART, 128) for part in range(PARTS)
    ]
    return jnp.concatenate(wide, axis=1)


def rank_weights(shape, axis, start):
    place = iota(shape, axis) - start
    weights = jnp.where(place == 0, 16384.0, jnp.where(place == 1, 128.0, 1.0))
    return jnp.where((place >= 0) & (place < 3), weights, 0.0).astype(jnp.bfloat16)


def homeward(best):
    stacked = jnp.concatenate(best, axis=0)
    widen = bits(iota((8, 128), 1) // HALF == iota((8, 128), 0))
    own_lane = iota((PART, 128), 1) % HALF == iota((PART, 128), 0) % HALF
    gather = bits(iota((GROUPS, PART), 1) // HALF == iota((GROUPS, PART), 0))
    total = jnp.zeros((GROUPS, 128), jnp.float32)
    for part in three_parts(stacked):
        lanes = jnp.where(own_lane, dot(part, widen, TN), 0.0).astype(jnp.bfloat16)
        total += dot(gather, lanes, NN)
    return total


def score_kernel(names, pairs, last, *refs):
    data = dict(zip(names, refs))
    carried = None if len(refs) == len(names) + 1 else refs[len(names)]
    out_ref = refs[-1]
    used = sorted({name for pair in pairs for name in pair[:2]})
    keys = {name: keys_of(data[name]) for name in used}
    by_row, by_lane = {}, {}
    for name in used:
        tile = data[name[0] + "0"][:, D // 8 :, :].reshape(PART, 128)
        start = 3 * int(name[1])
        by_row[name] = dot(tile, rank_weights((128, 128), 0, start), NN)
        by_lane[name] = dot(rank_weights((8, 128), 1, start), tile, NT)[0:1]
    best_row, best_lane = {}, {}
    for rows, columns, forward, backward in pairs:
        scores = dot(keys[rows], keys[columns], NT)
        row_rank = jnp.concatenate([by_row[rows]] * 4, axis=1)
        lane_rank = by_lane[columns]
        if forward:
            kept = jnp.where(lane_rank < row_rank, scores, -1.0)
            folded = functools.reduce(
                jnp.maximum, [kept[:, 128 * i : 128 * (i + 1)] for i in range(4)]
            )
            best_row[rows] = jnp.maximum(best_row[rows], folded) if rows in best_row else folded
        if backward:
            kept = jnp.where(row_rank < lane_rank, scores, -1.0)
            folded = jnp.max(kept, axis=0, keepdims=True)
            if columns in best_lane:
                folded = jnp.maximum(best_lane[columns], folded)
            best_lane[columns] = folded
    best = []
    for index, name in enumerate(FINALS):
        value = jnp.full((1, PART), -1.0) if carried is None else carried[index : index + 1, :]
        if name in best_lane:
            value = jnp.maximum(value, best_lane[name])
        if name in best_row:
            value = jnp.maximum(value, jnp.max(best_row[name].T, axis=0, keepdims=True))
        best.append(value)
    if last:
        out_ref[...] = homeward(best).reshape(GROUPS, 1, 128)
    else:
        out_ref[...] = jnp.concatenate(best, axis=0)


def score(blocks, pairs, carried, last, name):
    used = {half for pair in pairs for half in pair[:2]}
    names = tuple(sorted(used | {half[0] + "0" for half in used}))
    shape = ((GROUPS, 1, 128) if last else (8, PART), jnp.float32)
    operands = [blocks[half] for half in names] + ([] if carried is None else [carried])
    return call(
        functools.partial(score_kernel, names, pairs, last),
        name,
        [shape],
        *operands,
        flops=2 * len(pairs) * PART * PART * D,
    )


FIRST = (
    ("o0", "o0", True, False),
    ("o0", "s0", True, False),
    ("o0", "b0", True, True),
    ("s0", "b0", True, True),
    ("z0", "b0", True, True),
)
SECOND = (
    ("o1", "o1", True, False),
    ("o0", "o1", True, True),
    ("o1", "b0", True, True),
    ("o1", "s1", True, False),
    ("o0", "s1", True, True),
    ("s1", "b0", True, True),
)
THIRD = (
    ("o0", "b1", True, True),
    ("o1", "b1", True, True),
    ("s0", "b1", True, True),
    ("s1", "b1", True, True),
    ("z0", "b1", True, True),
    ("z1", "b0", True, True),
    ("z1", "b1", True, True),
)


def finish_kernel(own_ref, swap_ref, next_ref, last_ref, pos_ref, out_ref):
    block = iota((GROUPS, 128), 1) // SLOTS
    mine = last_ref[...].reshape(GROUPS, 128)
    for index, ref in enumerate((own_ref, swap_ref, next_ref)):
        mine = jnp.where(block == index, ref[...].reshape(GROUPS, 128), mine)
    position = pos_ref[...]
    member = bits(iota((GROUPS, ROWS), 0) == position // SLOTS)
    found = jnp.zeros((128, ROWS), jnp.float32)
    for part in three_parts(mine):
        found += dot(part, member, TN)
    best = functools.reduce(
        jnp.maximum, [found[SLOTS * index : SLOTS * (index + 1)] for index in range(4)]
    )
    here = iota((SLOTS, ROWS), 0) == (position & (SLOTS - 1))
    out_ref[...] = jnp.sum(jnp.where(here, best, 0.0), axis=0, keepdims=True)


FROM_NEXT = [
    (((x + 1) % 4) * 2 + (c if x < 2 else 1 - c), x * 2 + c) for x in range(4) for c in range(2)
]
FROM_LAST = [(((x - 1) % 4) * 2 + c, x * 2 + c) for x in range(4) for c in range(2)]
SWAP = [(x * 2 + 1 - c, x * 2 + c) for x in range(4) for c in range(2)]


def back(pairs):
    return [(there, here) for here, there in pairs]


def send(array, pairs):
    return lax.ppermute(array, ("x", "c"), pairs)


def to_home(array):
    return lax.all_to_all(array, ("y", "z"), split_axis=0, concat_axis=0, tiled=True)


def on_device(embeddings, cluster_ids, ranks):
    bf16 = jnp.bfloat16
    first, unit, position = call(
        pack_first,
        "pack_first",
        [((GROUPS, D // 8 + HALF, 128), bf16), ((ROWS, D), bf16), ((1, ROWS), jnp.int32)],
        embeddings,
        cluster_ids.reshape(1, ROWS),
        ranks.reshape(1, ROWS),
        flops=2 * PART * ROWS * D,
    )
    second = call(
        pack_second,
        "pack_second",
        [((GROUPS, D // 8, 128), bf16)],
        unit,
        position,
        flops=2 * PART * ROWS * D,
    )
    blocks = {}
    for half, packed in zip("01", (first, second)):
        blocks["o" + half] = home = to_home(packed)
        blocks["s" + half] = send(home, SWAP)
        blocks["b" + half] = send(home, FROM_NEXT)
        blocks["z" + half] = send(home, FROM_LAST)
    best = score(blocks, FIRST, None, False, "score_first")
    best = score(blocks, SECOND, best, False, "score_second")
    own = to_home(score(blocks, THIRD, best, True, "score_third"))
    nearest = call(
        finish_kernel,
        "finish",
        [((1, ROWS), jnp.float32)],
        own,
        send(own, back(SWAP)),
        send(own, back(FROM_NEXT)),
        send(own, back(FROM_LAST)),
        position,
    )
    return nearest.reshape(ROWS)


def solution(mesh):
    fine = Mesh(mesh.devices.reshape(tuple(SIZE.values())), tuple(SIZE))
    rows = P(tuple(SIZE))
    return jax.shard_map(
        on_device,
        mesh=fine,
        in_specs=(P(tuple(SIZE), None), P(tuple(SIZE), None), rows),
        out_specs=rows,
        check_vma=False,
    )
```

```python
import functools

import jax
import jax.numpy as jnp
from jax import lax
from jax.experimental import pallas as pl
from jax.experimental.pallas import tpu as pltpu
from jax.sharding import Mesh, PartitionSpec as P

D = 768
ROWS = 512
GROUPS = 32
HALF = 16
SLOTS = 2 * HALF
PART = GROUPS * HALF
PARTS = D // 128
SIZE = {"x": 4, "y": 4, "c": 2, "z": 8}
EARLY = 1
LIMIT = 24 * 1024 * 1024
NT = (((1,), (1,)), ((), ()))
NN = (((1,), (0,)), ((), ()))
TN = (((0,), (0,)), ((), ()))
BLOCKS = ("o", "s", "b", "z")
FINALS = tuple(block + half for block in BLOCKS for half in "01")


def dot(a, b, dims):
    return lax.dot_general(a, b, dims, preferred_element_type=jnp.float32)


def iota(shape, axis):
    return lax.broadcasted_iota(jnp.int32, shape, axis)


def bits(mask):
    return mask.astype(jnp.float32).astype(jnp.bfloat16)


def three_parts(value):
    parts = []
    for _ in range(3):
        part = value.astype(jnp.bfloat16)
        parts.append(part)
        value = value - part.astype(jnp.float32)
    return parts


def chosen_rows(position, half):
    slot, group = position & (SLOTS - 1), position // SLOTS
    row = jnp.where(slot // HALF == half, group * HALF + slot % HALF, -1)
    return bits(iota((PART, ROWS), 0) == row)


def put(moved, out_ref, start):
    moved = moved.astype(jnp.bfloat16)
    for part in range(moved.shape[1] // 128):
        rows = start + part * HALF
        out_ref[:, rows : rows + HALF, :] = moved[:, part * 128 : (part + 1) * 128].reshape(
            GROUPS, HALF, 128
        )


def pack_first(emb_ref, ids_ref, rank_ref, out_ref, unit_ref, pos_ref):
    rows = emb_ref[...]
    norms = jnp.sum(rows * rows, axis=1, keepdims=True)
    unit = (rows * lax.rsqrt(norms + 1e-06)).astype(jnp.bfloat16)
    unit_ref[...] = unit

    target = ids_ref[...]
    member = (iota((GROUPS, ROWS), 0) == target).astype(jnp.float32)
    earlier = bits(iota((ROWS, ROWS), 0) < iota((ROWS, ROWS), 1))
    before = dot(member.astype(jnp.bfloat16), earlier, NN)
    slot = jnp.sum(before * member, axis=0, keepdims=True).astype(jnp.int32)
    position = target * SLOTS + slot
    pos_ref[...] = position

    first, second = chosen_rows(position, 0), chosen_rows(position, 1)
    put(dot(first, unit, NN), out_ref, 0)
    put(dot(second, unit[:, : EARLY * 128], NN), out_ref, D // 8 + HALF)
    rank = rank_ref[...]
    line = iota((128, ROWS), 0)
    ranks = jnp.zeros((PART, 128), jnp.float32)
    for half, chosen in enumerate((first, second)):
        parts = jnp.zeros((128, ROWS), jnp.int32)
        for index, part in enumerate(((rank >> 14) - 128, (rank >> 7) & 127, rank & 127)):
            parts = jnp.where(line == 3 * half + index, part, parts)
        ranks += dot(chosen, parts.astype(jnp.float32).astype(jnp.bfloat16), NT)
    put(ranks, out_ref, D // 8)


def pack_second(unit_ref, pos_ref, out_ref):
    put(dot(chosen_rows(pos_ref[...], 1), unit_ref[:, EARLY * 128 :], NN), out_ref, 0)


def vmem(count):
    return [pl.BlockSpec(memory_space=pltpu.VMEM)] * count


def call(kernel, name, shapes, *operands, flops=0):
    shapes = tuple(jax.ShapeDtypeStruct(shape, dtype) for shape, dtype in shapes)
    out = pl.pallas_call(
        kernel,
        out_shape=shapes,
        in_specs=vmem(len(operands)),
        out_specs=tuple(vmem(len(shapes))),
        compiler_params=pltpu.CompilerParams(vmem_limit_bytes=LIMIT),
        cost_estimate=pl.CostEstimate(
            flops=flops,
            bytes_accessed=sum(array.size * array.dtype.itemsize for array in operands),
            transcendentals=0,
        ),
        name=name,
    )(*operands)
    return out[0] if len(shapes) == 1 else out


def tile(ref, index):
    return ref[:, index * HALF : (index + 1) * HALF, :].reshape(PART, 128)


def keys_of(data, name):
    first = data[name[0] + "0"]
    if name[1] == "0":
        wide = [tile(first, part) for part in range(PARTS)]
    else:
        wide = [tile(first, PARTS + 1 + part) for part in range(EARLY)]
        wide += [tile(data[name], part) for part in range(PARTS - EARLY)]
    return jnp.concatenate(wide, axis=1)


def rank_weights(shape, axis, start):
    place = iota(shape, axis) - start
    weights = jnp.where(place == 0, 16384.0, jnp.where(place == 1, 128.0, 1.0))
    return jnp.where((place >= 0) & (place < 3), weights, 0.0).astype(jnp.bfloat16)


def homeward(best):
    stacked = jnp.concatenate(best, axis=0)
    widen = bits(iota((8, 128), 1) // HALF == iota((8, 128), 0))
    own_lane = iota((PART, 128), 1) % HALF == iota((PART, 128), 0) % HALF
    gather = bits(iota((GROUPS, PART), 1) // HALF == iota((GROUPS, PART), 0))
    total = jnp.zeros((GROUPS, 128), jnp.float32)
    for part in three_parts(stacked):
        lanes = jnp.where(own_lane, dot(part, widen, TN), 0.0).astype(jnp.bfloat16)
        total += dot(gather, lanes, NN)
    return total


def score_kernel(names, pairs, last, *refs):
    data = dict(zip(names, refs))
    carried = None if len(refs) == len(names) + 1 else refs[len(names)]
    out_ref = refs[-1]
    used = sorted({name for pair in pairs for name in pair[:2]})
    keys = {name: keys_of(data, name) for name in used}
    by_row, by_lane = {}, {}
    for name in used:
        ranks = tile(data[name[0] + "0"], PARTS)
        start = 3 * int(name[1])
        by_row[name] = dot(ranks, rank_weights((128, 128), 0, start), NN)
        by_lane[name] = dot(rank_weights((8, 128), 1, start), ranks, NT)[0:1]
    best_row, best_lane = {}, {}
    for rows, columns, forward, backward in pairs:
        scores = dot(keys[rows], keys[columns], NT)
        row_rank = jnp.concatenate([by_row[rows]] * 4, axis=1)
        lane_rank = by_lane[columns]
        if forward:
            kept = jnp.where(lane_rank < row_rank, scores, -1.0)
            folded = functools.reduce(
                jnp.maximum, [kept[:, 128 * i : 128 * (i + 1)] for i in range(4)]
            )
            best_row[rows] = jnp.maximum(best_row[rows], folded) if rows in best_row else folded
        if backward:
            kept = jnp.where(row_rank < lane_rank, scores, -1.0)
            folded = jnp.max(kept, axis=0, keepdims=True)
            if columns in best_lane:
                folded = jnp.maximum(best_lane[columns], folded)
            best_lane[columns] = folded
    best = []
    for index, name in enumerate(FINALS):
        value = jnp.full((1, PART), -1.0) if carried is None else carried[index : index + 1, :]
        if name in best_lane:
            value = jnp.maximum(value, best_lane[name])
        if name in best_row:
            value = jnp.maximum(value, jnp.max(best_row[name].T, axis=0, keepdims=True))
        best.append(value)
    if last:
        out_ref[...] = homeward(best).reshape(GROUPS, 1, 128)
    else:
        out_ref[...] = jnp.concatenate(best, axis=0)


def score(blocks, pairs, carried, last, name):
    used = {half for pair in pairs for half in pair[:2]}
    names = tuple(sorted(used | {half[0] + "0" for half in used}))
    shape = ((GROUPS, 1, 128) if last else (8, PART), jnp.float32)
    operands = [blocks[half] for half in names] + ([] if carried is None else [carried])
    return call(
        functools.partial(score_kernel, names, pairs, last),
        name,
        [shape],
        *operands,
        flops=2 * len(pairs) * PART * PART * D,
    )


FIRST = (
    ("o0", "o0", True, False),
    ("o0", "s0", True, False),
    ("o0", "b0", True, True),
    ("s0", "b0", True, True),
    ("z0", "b0", True, True),
)
SECOND = (
    ("o1", "o1", True, False),
    ("o0", "o1", True, True),
    ("o1", "b0", True, True),
    ("o1", "s1", True, False),
    ("o0", "s1", True, True),
    ("s1", "b0", True, True),
    ("o1", "z0", True, True),
    ("s1", "z0", True, True),
)
THIRD = (
    ("o1", "b1", True, True),
    ("s1", "b1", True, True),
    ("z0", "b1", True, True),
    ("z1", "b0", True, True),
    ("z1", "b1", True, True),
)


def finish_kernel(own_ref, swap_ref, next_ref, last_ref, pos_ref, out_ref):
    block = iota((GROUPS, 128), 1) // SLOTS
    mine = last_ref[...].reshape(GROUPS, 128)
    for index, ref in enumerate((own_ref, swap_ref, next_ref)):
        mine = jnp.where(block == index, ref[...].reshape(GROUPS, 128), mine)
    position = pos_ref[...]
    member = bits(iota((GROUPS, ROWS), 0) == position // SLOTS)
    found = jnp.zeros((128, ROWS), jnp.float32)
    for part in three_parts(mine):
        found += dot(part, member, TN)
    best = functools.reduce(
        jnp.maximum, [found[SLOTS * index : SLOTS * (index + 1)] for index in range(4)]
    )
    here = iota((SLOTS, ROWS), 0) == (position & (SLOTS - 1))
    out_ref[...] = jnp.sum(jnp.where(here, best, 0.0), axis=0, keepdims=True)


FROM_NEXT = [
    (((x + 1) % 4) * 2 + (c if x < 2 else 1 - c), x * 2 + c) for x in range(4) for c in range(2)
]
FROM_LAST = [(((x - 1) % 4) * 2 + c, x * 2 + c) for x in range(4) for c in range(2)]
SWAP = [(x * 2 + 1 - c, x * 2 + c) for x in range(4) for c in range(2)]


def back(pairs):
    return [(there, here) for here, there in pairs]


def send(array, pairs):
    return lax.ppermute(array, ("x", "c"), pairs)


def to_home(array):
    return lax.all_to_all(array, ("y", "z"), split_axis=0, concat_axis=0, tiled=True)


def on_device(embeddings, cluster_ids, ranks):
    bf16 = jnp.bfloat16
    first, unit, position = call(
        pack_first,
        "pack_first",
        [((GROUPS, D // 8 + (1 + EARLY) * HALF, 128), bf16), ((ROWS, D), bf16), ((1, ROWS), jnp.int32)],
        embeddings,
        cluster_ids.reshape(1, ROWS),
        ranks.reshape(1, ROWS),
        flops=2 * PART * ROWS * D,
    )
    second = call(
        pack_second,
        "pack_second",
        [((GROUPS, D // 8 - EARLY * HALF, 128), bf16)],
        unit,
        position,
        flops=2 * PART * ROWS * D,
    )
    blocks = {}
    for half, packed in zip("01", (first, second)):
        blocks["o" + half] = home = to_home(packed)
        blocks["s" + half] = send(home, SWAP)
        blocks["b" + half] = send(home, FROM_NEXT)
        blocks["z" + half] = send(home, FROM_LAST)
    best = score(blocks, FIRST, None, False, "score_first")
    best = score(blocks, SECOND, best, False, "score_second")
    own = to_home(score(blocks, THIRD, best, True, "score_third"))
    nearest = call(
        finish_kernel,
        "finish",
        [((1, ROWS), jnp.float32)],
        own,
        send(own, back(SWAP)),
        send(own, back(FROM_NEXT)),
        send(own, back(FROM_LAST)),
        position,
    )
    return nearest.reshape(ROWS)


def solution(mesh):
    fine = Mesh(mesh.devices.reshape(tuple(SIZE.values())), tuple(SIZE))
    rows = P(tuple(SIZE))
    return jax.shard_map(
        on_device,
        mesh=fine,
        in_specs=(P(tuple(SIZE), None), P(tuple(SIZE), None), rows),
        out_specs=rows,
        check_vma=False,
    )
```

```python
import functools

import jax
import jax.numpy as jnp
from jax import lax
from jax.experimental import pallas as pl
from jax.experimental.pallas import tpu as pltpu
from jax.sharding import Mesh, PartitionSpec as P

D = 768
ROWS = 512
GROUPS = 32
HALF = 16
SLOTS = 2 * HALF
PART = GROUPS * HALF
PARTS = D // 128
SIZE = {"x": 4, "y": 4, "c": 2, "z": 8}
EARLY = 0
CUTS = 4
LIMIT = 24 * 1024 * 1024
NT = (((1,), (1,)), ((), ()))
NN = (((1,), (0,)), ((), ()))
TN = (((0,), (0,)), ((), ()))
BLOCKS = ("o", "s", "b", "z")
FINALS = tuple(block + half for block in BLOCKS for half in "01")


def dot(a, b, dims):
    return lax.dot_general(a, b, dims, preferred_element_type=jnp.float32)


def iota(shape, axis):
    return lax.broadcasted_iota(jnp.int32, shape, axis)


def bits(mask):
    return mask.astype(jnp.float32).astype(jnp.bfloat16)


def three_parts(value):
    parts = []
    for _ in range(3):
        part = value.astype(jnp.bfloat16)
        parts.append(part)
        value = value - part.astype(jnp.float32)
    return parts


def chosen_rows(position, half):
    slot, group = position & (SLOTS - 1), position // SLOTS
    row = jnp.where(slot // HALF == half, group * HALF + slot % HALF, -1)
    return bits(iota((PART, ROWS), 0) == row)


def put(moved, out_ref, start):
    moved = moved.astype(jnp.bfloat16)
    for part in range(moved.shape[1] // 128):
        rows = start + part * HALF
        out_ref[:, rows : rows + HALF, :] = moved[:, part * 128 : (part + 1) * 128].reshape(
            GROUPS, HALF, 128
        )


def pack_first(emb_hbm, ids_hbm, rank_hbm, out_ref, unit_ref, pos_ref, emb_ref, ids_ref, rank_ref, sems):
    pieces = [pl.ds(start, ROWS // CUTS) for start in range(0, ROWS, ROWS // CUTS)]
    copies = [
        pltpu.make_async_copy(ids_hbm, ids_ref, sems.at[CUTS]),
        pltpu.make_async_copy(rank_hbm, rank_ref, sems.at[CUTS + 1]),
    ] + [
        pltpu.make_async_copy(emb_hbm.at[piece], emb_ref.at[piece], sems.at[index])
        for index, piece in enumerate(pieces)
    ]
    for copy in copies:
        copy.start()
    for copy in copies[:2]:
        copy.wait()

    target = ids_ref[...]
    member = (iota((GROUPS, ROWS), 0) == target).astype(jnp.float32)
    earlier = bits(iota((ROWS, ROWS), 0) < iota((ROWS, ROWS), 1))
    before = dot(member.astype(jnp.bfloat16), earlier, NN)
    slot = jnp.sum(before * member, axis=0, keepdims=True).astype(jnp.int32)
    position = target * SLOTS + slot
    pos_ref[...] = position

    first, second = chosen_rows(position, 0), chosen_rows(position, 1)
    for copy, piece in zip(copies[2:], pieces):
        copy.wait()
        rows = emb_ref[piece, :]
        norms = jnp.sum(rows * rows, axis=1, keepdims=True)
        unit_ref[piece, :] = (rows * lax.rsqrt(norms + 1e-06)).astype(jnp.bfloat16)
    unit = unit_ref[...]
    put(dot(first, unit, NN), out_ref, 0)
    if EARLY:
        put(dot(second, unit[:, : EARLY * 128], NN), out_ref, D // 8 + HALF)
    rank = rank_ref[...]
    line = iota((128, ROWS), 0)
    ranks = jnp.zeros((PART, 128), jnp.float32)
    for half, chosen in enumerate((first, second)):
        parts = jnp.zeros((128, ROWS), jnp.int32)
        for index, part in enumerate(((rank >> 14) - 128, (rank >> 7) & 127, rank & 127)):
            parts = jnp.where(line == 3 * half + index, part, parts)
        ranks += dot(chosen, parts.astype(jnp.float32).astype(jnp.bfloat16), NT)
    put(ranks, out_ref, D // 8)


def pack_second(unit_ref, pos_ref, out_ref):
    put(dot(chosen_rows(pos_ref[...], 1), unit_ref[:, EARLY * 128 :], NN), out_ref, 0)


def vmem(count):
    return [pl.BlockSpec(memory_space=pltpu.VMEM)] * count


def call(kernel, name, shapes, *operands, flops=0, scratch=None, limit=LIMIT):
    shapes = tuple(jax.ShapeDtypeStruct(shape, dtype) for shape, dtype in shapes)
    out = pl.pallas_call(
        kernel,
        out_shape=shapes,
        in_specs=[pl.BlockSpec(memory_space=pltpu.HBM)] * len(operands) if scratch else vmem(len(operands)),
        out_specs=tuple(vmem(len(shapes))),
        scratch_shapes=scratch or [],
        compiler_params=pltpu.CompilerParams(vmem_limit_bytes=limit),
        cost_estimate=pl.CostEstimate(
            flops=flops,
            bytes_accessed=sum(array.size * array.dtype.itemsize for array in operands),
            transcendentals=0,
        ),
        name=name,
    )(*operands)
    return out[0] if len(shapes) == 1 else out


def tile(ref, index):
    return ref[:, index * HALF : (index + 1) * HALF, :].reshape(PART, 128)


def keys_of(data, name):
    first = data[name[0] + "0"]
    if name[1] == "0":
        wide = [tile(first, part) for part in range(PARTS)]
    else:
        wide = [tile(first, PARTS + 1 + part) for part in range(EARLY)]
        wide += [tile(data[name], part) for part in range(PARTS - EARLY)]
    return jnp.concatenate(wide, axis=1)


def rank_weights(shape, axis, start):
    place = iota(shape, axis) - start
    weights = jnp.where(place == 0, 16384.0, jnp.where(place == 1, 128.0, 1.0))
    return jnp.where((place >= 0) & (place < 3), weights, 0.0).astype(jnp.bfloat16)


def homeward(best):
    stacked = jnp.concatenate(best, axis=0)
    widen = bits(iota((8, 128), 1) // HALF == iota((8, 128), 0))
    own_lane = iota((PART, 128), 1) % HALF == iota((PART, 128), 0) % HALF
    gather = bits(iota((GROUPS, PART), 1) // HALF == iota((GROUPS, PART), 0))
    total = jnp.zeros((GROUPS, 128), jnp.float32)
    for part in three_parts(stacked):
        lanes = jnp.where(own_lane, dot(part, widen, TN), 0.0).astype(jnp.bfloat16)
        total += dot(gather, lanes, NN)
    return total


def score_kernel(names, pairs, last, *refs):
    data = dict(zip(names, refs))
    carried = None if len(refs) == len(names) + 1 else refs[len(names)]
    out_ref = refs[-1]
    used = sorted({name for pair in pairs for name in pair[:2]})
    keys = {name: keys_of(data, name) for name in used}
    by_row, by_lane = {}, {}
    for name in used:
        ranks = tile(data[name[0] + "0"], PARTS)
        start = 3 * int(name[1])
        by_row[name] = dot(ranks, rank_weights((128, 128), 0, start), NN)
        by_lane[name] = dot(rank_weights((8, 128), 1, start), ranks, NT)[0:1]
    best_row, best_lane = {}, {}
    for rows, columns, forward, backward in pairs:
        scores = dot(keys[rows], keys[columns], NT)
        row_rank = jnp.concatenate([by_row[rows]] * 4, axis=1)
        lane_rank = by_lane[columns]
        if forward:
            kept = jnp.where(lane_rank < row_rank, scores, -1.0)
            folded = functools.reduce(
                jnp.maximum, [kept[:, 128 * i : 128 * (i + 1)] for i in range(4)]
            )
            best_row[rows] = jnp.maximum(best_row[rows], folded) if rows in best_row else folded
        if backward:
            kept = jnp.where(row_rank < lane_rank, scores, -1.0)
            folded = jnp.max(kept, axis=0, keepdims=True)
            if columns in best_lane:
                folded = jnp.maximum(best_lane[columns], folded)
            best_lane[columns] = folded
    best = []
    for index, name in enumerate(FINALS):
        value = jnp.full((1, PART), -1.0) if carried is None else carried[index : index + 1, :]
        if name in best_lane:
            value = jnp.maximum(value, best_lane[name])
        if name in best_row:
            value = jnp.maximum(value, jnp.max(best_row[name].T, axis=0, keepdims=True))
        best.append(value)
    if last:
        out_ref[...] = homeward(best).reshape(GROUPS, 1, 128)
    else:
        out_ref[...] = jnp.concatenate(best, axis=0)


def score(blocks, pairs, carried, last, name):
    used = {half for pair in pairs for half in pair[:2]}
    names = tuple(sorted(used | {half[0] + "0" for half in used}))
    shape = ((GROUPS, 1, 128) if last else (8, PART), jnp.float32)
    operands = [blocks[half] for half in names] + ([] if carried is None else [carried])
    return call(
        functools.partial(score_kernel, names, pairs, last),
        name,
        [shape],
        *operands,
        flops=2 * len(pairs) * PART * PART * D,
    )


FIRST = (
    ("o0", "o0", True, False),
    ("o0", "s0", True, False),
    ("o0", "b0", True, True),
    ("s0", "b0", True, True),
    ("z0", "b0", True, True),
)
SECOND = (
    ("o1", "o1", True, False),
    ("o0", "o1", True, True),
    ("o1", "b0", True, True),
    ("o1", "s1", True, False),
    ("o0", "s1", True, True),
    ("s1", "b0", True, True),
    ("o1", "z0", True, True),
    ("s1", "z0", True, True),
)
THIRD = (
    ("o1", "b1", True, True),
    ("s1", "b1", True, True),
    ("z0", "b1", True, True),
    ("z1", "b0", True, True),
    ("z1", "b1", True, True),
)


def finish_kernel(own_ref, swap_ref, next_ref, last_ref, pos_ref, out_ref):
    block = iota((GROUPS, 128), 1) // SLOTS
    mine = last_ref[...].reshape(GROUPS, 128)
    for index, ref in enumerate((own_ref, swap_ref, next_ref)):
        mine = jnp.where(block == index, ref[...].reshape(GROUPS, 128), mine)
    position = pos_ref[...]
    member = bits(iota((GROUPS, ROWS), 0) == position // SLOTS)
    found = jnp.zeros((128, ROWS), jnp.float32)
    for part in three_parts(mine):
        found += dot(part, member, TN)
    best = functools.reduce(
        jnp.maximum, [found[SLOTS * index : SLOTS * (index + 1)] for index in range(4)]
    )
    here = iota((SLOTS, ROWS), 0) == (position & (SLOTS - 1))
    out_ref[...] = jnp.sum(jnp.where(here, best, 0.0), axis=0, keepdims=True)


FROM_NEXT = [
    (((x + 1) % 4) * 2 + (c if x < 2 else 1 - c), x * 2 + c) for x in range(4) for c in range(2)
]
FROM_LAST = [(((x - 1) % 4) * 2 + c, x * 2 + c) for x in range(4) for c in range(2)]
SWAP = [(x * 2 + 1 - c, x * 2 + c) for x in range(4) for c in range(2)]


def back(pairs):
    return [(there, here) for here, there in pairs]


def send(array, pairs):
    return lax.ppermute(array, ("x", "c"), pairs)


def to_home(array):
    return lax.all_to_all(array, ("y", "z"), split_axis=0, concat_axis=0, tiled=True)


def on_device(embeddings, cluster_ids, ranks):
    bf16 = jnp.bfloat16
    first, unit, position = call(
        pack_first,
        "pack_first",
        [((GROUPS, D // 8 + (1 + EARLY) * HALF, 128), bf16), ((ROWS, D), bf16), ((1, ROWS), jnp.int32)],
        embeddings,
        cluster_ids.reshape(1, ROWS),
        ranks.reshape(1, ROWS),
        flops=2 * PART * ROWS * D,
        scratch=[
            pltpu.VMEM((ROWS, D), jnp.float32),
            pltpu.VMEM((1, ROWS), jnp.int32),
            pltpu.VMEM((1, ROWS), jnp.int32),
            pltpu.SemaphoreType.DMA((CUTS + 2,)),
        ],
        limit=60 * 1024 * 1024,
    )
    second = call(
        pack_second,
        "pack_second",
        [((GROUPS, D // 8 - EARLY * HALF, 128), bf16)],
        unit,
        position,
        flops=2 * PART * ROWS * D,
    )
    blocks = {}
    for half, packed in zip("01", (first, second)):
        blocks["o" + half] = home = to_home(packed)
        blocks["s" + half] = send(home, SWAP)
        blocks["b" + half] = send(home, FROM_NEXT)
        blocks["z" + half] = send(home, FROM_LAST)
    best = score(blocks, FIRST, None, False, "score_first")
    best = score(blocks, SECOND, best, False, "score_second")
    own = to_home(score(blocks, THIRD, best, True, "score_third"))
    nearest = call(
        finish_kernel,
        "finish",
        [((1, ROWS), jnp.float32)],
        own,
        send(own, back(SWAP)),
        send(own, back(FROM_NEXT)),
        send(own, back(FROM_LAST)),
        position,
    )
    return nearest.reshape(ROWS)


def solution(mesh):
    fine = Mesh(mesh.devices.reshape(tuple(SIZE.values())), tuple(SIZE))
    rows = P(tuple(SIZE))
    return jax.shard_map(
        on_device,
        mesh=fine,
        in_specs=(P(tuple(SIZE), None), P(tuple(SIZE), None), rows),
        out_specs=rows,
        check_vma=False,
    )
```

```python
import functools

import jax
import jax.numpy as jnp
from jax import lax
from jax.experimental import pallas as pl
from jax.experimental.pallas import tpu as pltpu
from jax.sharding import Mesh, PartitionSpec as P

D = 768
ROWS = 512
GROUPS = 32
HALF = 16
SLOTS = 2 * HALF
PART = GROUPS * HALF
PARTS = D // 128
SIZE = {"x": 4, "y": 4, "c": 2, "z": 8}
EARLY = 0
CUTS = 4
LIMIT = 24 * 1024 * 1024
NT = (((1,), (1,)), ((), ()))
NN = (((1,), (0,)), ((), ()))
TN = (((0,), (0,)), ((), ()))
BLOCKS = ("o", "s", "b", "z")
FINALS = tuple(block + half for block in BLOCKS for half in "01")


def dot(a, b, dims):
    return lax.dot_general(a, b, dims, preferred_element_type=jnp.float32)


def iota(shape, axis):
    return lax.broadcasted_iota(jnp.int32, shape, axis)


def bits(mask):
    return mask.astype(jnp.float32).astype(jnp.bfloat16)


def three_parts(value):
    parts = []
    for _ in range(3):
        part = value.astype(jnp.bfloat16)
        parts.append(part)
        value = value - part.astype(jnp.float32)
    return parts


def chosen_rows(position, half):
    slot, group = position & (SLOTS - 1), position // SLOTS
    row = jnp.where(slot // HALF == half, group * HALF + slot % HALF, -1)
    return bits(iota((PART, ROWS), 0) == row)


def put(moved, out_ref, start):
    moved = moved.astype(jnp.bfloat16)
    for part in range(moved.shape[1] // 128):
        rows = start + part * HALF
        out_ref[:, rows : rows + HALF, :] = moved[:, part * 128 : (part + 1) * 128].reshape(
            GROUPS, HALF, 128
        )


def pack_first(emb_hbm, ids_hbm, rank_hbm, out_ref, unit_ref, pos_ref, emb_ref, ids_ref, rank_ref, sems):
    pieces = [pl.ds(start, ROWS // CUTS) for start in range(0, ROWS, ROWS // CUTS)]
    copies = [
        pltpu.make_async_copy(ids_hbm, ids_ref, sems.at[CUTS]),
        pltpu.make_async_copy(rank_hbm, rank_ref, sems.at[CUTS + 1]),
    ] + [
        pltpu.make_async_copy(emb_hbm.at[piece], emb_ref.at[piece], sems.at[index])
        for index, piece in enumerate(pieces)
    ]
    for copy in copies:
        copy.start()
    for copy in copies[:2]:
        copy.wait()

    target = ids_ref[...]
    member = (iota((GROUPS, ROWS), 0) == target).astype(jnp.float32)
    earlier = bits(iota((ROWS, ROWS), 0) < iota((ROWS, ROWS), 1))
    before = dot(member.astype(jnp.bfloat16), earlier, NN)
    slot = jnp.sum(before * member, axis=0, keepdims=True).astype(jnp.int32)
    position = target * SLOTS + slot
    pos_ref[...] = position

    first, second = chosen_rows(position, 0), chosen_rows(position, 1)
    for copy, piece in zip(copies[2:], pieces):
        copy.wait()
        rows = emb_ref[piece, :]
        norms = jnp.sum(rows * rows, axis=1, keepdims=True)
        unit_ref[piece, :] = (rows * lax.rsqrt(norms + 1e-06)).astype(jnp.bfloat16)
    unit = unit_ref[...]
    put(dot(first, unit, NN), out_ref, 0)
    if EARLY:
        put(dot(second, unit[:, : EARLY * 128], NN), out_ref, D // 8 + HALF)
    rank = rank_ref[...]
    line = iota((128, ROWS), 0)
    ranks = jnp.zeros((PART, 128), jnp.float32)
    for half, chosen in enumerate((first, second)):
        parts = jnp.zeros((128, ROWS), jnp.int32)
        for index, part in enumerate(((rank >> 14) - 128, (rank >> 7) & 127, rank & 127)):
            parts = jnp.where(line == 3 * half + index, part, parts)
        ranks += dot(chosen, parts.astype(jnp.float32).astype(jnp.bfloat16), NT)
    put(ranks, out_ref, D // 8)


def pack_second(unit_ref, pos_ref, out_ref):
    put(dot(chosen_rows(pos_ref[...], 1), unit_ref[:, EARLY * 128 :], NN), out_ref, 0)


def vmem(count):
    return [pl.BlockSpec(memory_space=pltpu.VMEM)] * count


def call(kernel, name, shapes, *operands, flops=0, scratch=None, limit=LIMIT):
    shapes = tuple(jax.ShapeDtypeStruct(shape, dtype) for shape, dtype in shapes)
    out = pl.pallas_call(
        kernel,
        out_shape=shapes,
        in_specs=[pl.BlockSpec(memory_space=pltpu.HBM)] * len(operands) if scratch else vmem(len(operands)),
        out_specs=tuple(vmem(len(shapes))),
        scratch_shapes=scratch or [],
        compiler_params=pltpu.CompilerParams(vmem_limit_bytes=limit),
        cost_estimate=pl.CostEstimate(
            flops=flops,
            bytes_accessed=sum(array.size * array.dtype.itemsize for array in operands),
            transcendentals=0,
        ),
        name=name,
    )(*operands)
    return out[0] if len(shapes) == 1 else out


def tile(ref, index):
    return ref[:, index * HALF : (index + 1) * HALF, :].reshape(PART, 128)


def keys_of(data, name):
    first = data[name[0] + "0"]
    if name[1] == "0":
        wide = [tile(first, part) for part in range(PARTS)]
    else:
        wide = [tile(first, PARTS + 1 + part) for part in range(EARLY)]
        wide += [tile(data[name], part) for part in range(PARTS - EARLY)]
    return jnp.concatenate(wide, axis=1)


def rank_weights(shape, axis, start):
    place = iota(shape, axis) - start
    weights = jnp.where(place == 0, 16384.0, jnp.where(place == 1, 128.0, 1.0))
    return jnp.where((place >= 0) & (place < 3), weights, 0.0).astype(jnp.bfloat16)


def homeward(best):
    stacked = jnp.concatenate(best, axis=0)
    widen = bits(iota((8, 128), 1) // HALF == iota((8, 128), 0))
    own_lane = iota((PART, 128), 1) % HALF == iota((PART, 128), 0) % HALF
    gather = bits(iota((GROUPS, PART), 1) // HALF == iota((GROUPS, PART), 0))
    total = jnp.zeros((GROUPS, 128), jnp.float32)
    for part in three_parts(stacked):
        lanes = jnp.where(own_lane, dot(part, widen, TN), 0.0).astype(jnp.bfloat16)
        total += dot(gather, lanes, NN)
    return total


def score_kernel(names, pairs, last, *refs):
    data = dict(zip(names, refs))
    refs = refs[len(names) :]
    if pairs is FIRST:
        carried, (out_ref, keep_ref) = None, refs
        keep_ref[...] = data["b0"][...]
    else:
        carried, out_ref = refs
    used = sorted({name for pair in pairs for name in pair[:2]})
    keys = {name: keys_of(data, name) for name in used}
    by_row, by_lane = {}, {}
    for name in used:
        ranks = tile(data[name[0] + "0"], PARTS)
        start = 3 * int(name[1])
        by_row[name] = dot(ranks, rank_weights((128, 128), 0, start), NN)
        by_lane[name] = dot(rank_weights((8, 128), 1, start), ranks, NT)[0:1]
    best_row, best_lane = {}, {}
    for rows, columns, forward, backward in pairs:
        scores = dot(keys[rows], keys[columns], NT)
        row_rank = jnp.concatenate([by_row[rows]] * 4, axis=1)
        lane_rank = by_lane[columns]
        if forward:
            kept = jnp.where(lane_rank < row_rank, scores, -1.0)
            folded = functools.reduce(
                jnp.maximum, [kept[:, 128 * i : 128 * (i + 1)] for i in range(4)]
            )
            best_row[rows] = jnp.maximum(best_row[rows], folded) if rows in best_row else folded
        if backward:
            kept = jnp.where(row_rank < lane_rank, scores, -1.0)
            folded = jnp.max(kept, axis=0, keepdims=True)
            if columns in best_lane:
                folded = jnp.maximum(best_lane[columns], folded)
            best_lane[columns] = folded
    best = []
    for index, name in enumerate(FINALS):
        value = jnp.full((1, PART), -1.0) if carried is None else carried[index : index + 1, :]
        if name in best_lane:
            value = jnp.maximum(value, best_lane[name])
        if name in best_row:
            value = jnp.maximum(value, jnp.max(best_row[name].T, axis=0, keepdims=True))
        best.append(value)
    if last:
        out_ref[...] = homeward(best).reshape(GROUPS, 1, 128)
    else:
        out_ref[...] = jnp.concatenate(best, axis=0)


def score(blocks, pairs, carried, last, name):
    used = {half for pair in pairs for half in pair[:2]}
    names = tuple(sorted(used | {half[0] + "0" for half in used}))
    shape = ((GROUPS, 1, 128) if last else (8, PART), jnp.float32)
    shapes = [shape]
    if pairs is FIRST:
        shapes.append((blocks["b0"].shape, blocks["b0"].dtype))
    operands = [blocks[half] for half in names] + ([] if carried is None else [carried])
    return call(
        functools.partial(score_kernel, names, pairs, last),
        name,
        shapes,
        *operands,
        flops=2 * len(pairs) * PART * PART * D,
    )


FIRST = (
    ("o0", "o0", True, False),
    ("o0", "s0", True, False),
    ("o0", "b0", True, True),
    ("s0", "b0", True, True),
    ("z0", "b0", True, True),
)
SECOND = (
    ("o1", "o1", True, False),
    ("o0", "o1", True, True),
    ("o1", "b0", True, True),
    ("o1", "s1", True, False),
    ("o0", "s1", True, True),
    ("s1", "b0", True, True),
    ("o1", "z0", True, True),
    ("s1", "z0", True, True),
)
THIRD = (
    ("o1", "b1", True, True),
    ("s1", "b1", True, True),
    ("z0", "b1", True, True),
    ("z1", "b0", True, True),
    ("z1", "b1", True, True),
)


def finish_kernel(own_ref, swap_ref, next_ref, last_ref, pos_ref, out_ref):
    block = iota((GROUPS, 128), 1) // SLOTS
    mine = last_ref[...].reshape(GROUPS, 128)
    for index, ref in enumerate((own_ref, swap_ref, next_ref)):
        mine = jnp.where(block == index, ref[...].reshape(GROUPS, 128), mine)
    position = pos_ref[...]
    member = bits(iota((GROUPS, ROWS), 0) == position // SLOTS)
    found = jnp.zeros((128, ROWS), jnp.float32)
    for part in three_parts(mine):
        found += dot(part, member, TN)
    best = functools.reduce(
        jnp.maximum, [found[SLOTS * index : SLOTS * (index + 1)] for index in range(4)]
    )
    here = iota((SLOTS, ROWS), 0) == (position & (SLOTS - 1))
    out_ref[...] = jnp.sum(jnp.where(here, best, 0.0), axis=0, keepdims=True)


FROM_NEXT = [
    (((x + 1) % 4) * 2 + (c if x < 2 else 1 - c), x * 2 + c) for x in range(4) for c in range(2)
]
FROM_LAST = [(((x - 1) % 4) * 2 + c, x * 2 + c) for x in range(4) for c in range(2)]
SWAP = [(x * 2 + 1 - c, x * 2 + c) for x in range(4) for c in range(2)]


def back(pairs):
    return [(there, here) for here, there in pairs]


def send(array, pairs):
    return lax.ppermute(array, ("x", "c"), pairs)


def to_home(array):
    return lax.all_to_all(array, ("y", "z"), split_axis=0, concat_axis=0, tiled=True)


def on_device(embeddings, cluster_ids, ranks):
    bf16 = jnp.bfloat16
    first, unit, position = call(
        pack_first,
        "pack_first",
        [((GROUPS, D // 8 + (1 + EARLY) * HALF, 128), bf16), ((ROWS, D), bf16), ((1, ROWS), jnp.int32)],
        embeddings,
        cluster_ids.reshape(1, ROWS),
        ranks.reshape(1, ROWS),
        flops=2 * PART * ROWS * D,
        scratch=[
            pltpu.VMEM((ROWS, D), jnp.float32),
            pltpu.VMEM((1, ROWS), jnp.int32),
            pltpu.VMEM((1, ROWS), jnp.int32),
            pltpu.SemaphoreType.DMA((CUTS + 2,)),
        ],
        limit=60 * 1024 * 1024,
    )
    second = call(
        pack_second,
        "pack_second",
        [((GROUPS, D // 8 - EARLY * HALF, 128), bf16)],
        unit,
        position,
        flops=2 * PART * ROWS * D,
    )
    blocks = {}
    for half, packed in zip("01", (first, second)):
        blocks["o" + half] = home = to_home(packed)
        blocks["s" + half] = send(home, SWAP)
        blocks["b" + half] = send(home, FROM_NEXT)
        blocks["z" + half] = send(home, FROM_LAST)
    best, blocks["b0"] = score(blocks, FIRST, None, False, "score_first")
    best = score(blocks, SECOND, best, False, "score_second")
    own = to_home(score(blocks, THIRD, best, True, "score_third"))
    nearest = call(
        finish_kernel,
        "finish",
        [((1, ROWS), jnp.float32)],
        own,
        send(own, back(SWAP)),
        send(own, back(FROM_NEXT)),
        send(own, back(FROM_LAST)),
        position,
    )
    return nearest.reshape(ROWS)


def solution(mesh):
    fine = Mesh(mesh.devices.reshape(tuple(SIZE.values())), tuple(SIZE))
    rows = P(tuple(SIZE))
    return jax.shard_map(
        on_device,
        mesh=fine,
        in_specs=(P(tuple(SIZE), None), P(tuple(SIZE), None), rows),
        out_specs=rows,
        check_vma=False,
    )
```

```python
import functools

import jax
import jax.numpy as jnp
from jax import lax
from jax.experimental import pallas as pl
from jax.experimental.pallas import tpu as pltpu
from jax.sharding import Mesh, PartitionSpec as P

D = 768
ROWS = 512
GROUPS = 32
HALF = 16
SLOTS = 2 * HALF
PART = GROUPS * HALF
PARTS = D // 128
SIZE = {"x": 4, "y": 4, "c": 2, "z": 8}
EARLY = 1
CUTS = 4
LIMIT = 24 * 1024 * 1024
NT = (((1,), (1,)), ((), ()))
NN = (((1,), (0,)), ((), ()))
TN = (((0,), (0,)), ((), ()))
BLOCKS = ("o", "s", "b", "z")
KEPT = ("b0", "z0")
FINALS = tuple(block + half for block in BLOCKS for half in "01")


def dot(a, b, dims):
    return lax.dot_general(a, b, dims, preferred_element_type=jnp.float32)


def iota(shape, axis):
    return lax.broadcasted_iota(jnp.int32, shape, axis)


def bits(mask):
    return mask.astype(jnp.float32).astype(jnp.bfloat16)


def three_parts(value):
    parts = []
    for _ in range(3):
        part = value.astype(jnp.bfloat16)
        parts.append(part)
        value = value - part.astype(jnp.float32)
    return parts


def chosen_rows(position, half):
    slot, group = position & (SLOTS - 1), position // SLOTS
    row = jnp.where(slot // HALF == half, group * HALF + slot % HALF, -1)
    return bits(iota((PART, ROWS), 0) == row)


def put(moved, out_ref, start):
    moved = moved.astype(jnp.bfloat16)
    for part in range(moved.shape[1] // 128):
        rows = start + part * HALF
        out_ref[:, rows : rows + HALF, :] = moved[:, part * 128 : (part + 1) * 128].reshape(
            GROUPS, HALF, 128
        )


def pack_first(
    emb_hbm, ids_hbm, rank_hbm, out_ref, table_ref, unit_ref, pos_ref, emb_ref, ids_ref, rank_ref, sems
):
    pieces = [pl.ds(start, ROWS // CUTS) for start in range(0, ROWS, ROWS // CUTS)]
    copies = [
        pltpu.make_async_copy(ids_hbm, ids_ref, sems.at[CUTS]),
        pltpu.make_async_copy(rank_hbm, rank_ref, sems.at[CUTS + 1]),
    ] + [
        pltpu.make_async_copy(emb_hbm.at[piece], emb_ref.at[piece], sems.at[index])
        for index, piece in enumerate(pieces)
    ]
    for copy in copies:
        copy.start()
    for copy in copies[:2]:
        copy.wait()

    target = ids_ref[...]
    member = (iota((GROUPS, ROWS), 0) == target).astype(jnp.float32)
    earlier = bits(iota((ROWS, ROWS), 0) < iota((ROWS, ROWS), 1))
    before = dot(member.astype(jnp.bfloat16), earlier, NN)
    slot = jnp.sum(before * member, axis=0, keepdims=True).astype(jnp.int32)
    position = target * SLOTS + slot
    pos_ref[...] = position

    first, second = chosen_rows(position, 0), chosen_rows(position, 1)
    for copy, piece in zip(copies[2:], pieces):
        copy.wait()
        rows = emb_ref[piece, :]
        norms = jnp.sum(rows * rows, axis=1, keepdims=True)
        unit_ref[piece, :] = (rows * lax.rsqrt(norms + 1e-06)).astype(jnp.bfloat16)
    unit = unit_ref[...]
    put(dot(first, unit, NN), out_ref, 0)
    if EARLY:
        put(dot(second, unit[:, : EARLY * 128], NN), out_ref, D // 8)
    rank = rank_ref[...]
    line = iota((128, ROWS), 0)
    ranks = jnp.zeros((PART, 128), jnp.float32)
    for half, chosen in enumerate((first, second)):
        parts = jnp.zeros((128, ROWS), jnp.int32)
        for index, part in enumerate(((rank >> 14) - 128, (rank >> 7) & 127, rank & 127)):
            parts = jnp.where(line == 3 * half + index, part, parts)
        ranks += dot(chosen, parts.astype(jnp.float32).astype(jnp.bfloat16), NT)
    put(ranks, table_ref, 0)


def pack_second(unit_ref, pos_ref, *refs):
    out_ref = refs[-1]
    put(dot(chosen_rows(pos_ref[...], 1), unit_ref[:, EARLY * 128 :], NN), out_ref, 0)
    ranks = jnp.zeros((PART, 128), jnp.float32)
    lane, other = iota((128, 128), 0), iota((128, 128), 1)
    for index, table_ref in enumerate(refs[:-1]):
        moved = bits((lane < 6) & (other == lane + 6 * index))
        ranks += dot(tile(table_ref, 0), moved, NN)
    put(ranks, out_ref, D // 8 - EARLY * HALF)


def vmem(count):
    return [pl.BlockSpec(memory_space=pltpu.VMEM)] * count


def call(kernel, name, shapes, *operands, flops=0, scratch=None, limit=LIMIT):
    shapes = tuple(jax.ShapeDtypeStruct(shape, dtype) for shape, dtype in shapes)
    out = pl.pallas_call(
        kernel,
        out_shape=shapes,
        in_specs=[pl.BlockSpec(memory_space=pltpu.HBM)] * len(operands) if scratch else vmem(len(operands)),
        out_specs=tuple(vmem(len(shapes))),
        scratch_shapes=scratch or [],
        compiler_params=pltpu.CompilerParams(vmem_limit_bytes=limit),
        cost_estimate=pl.CostEstimate(
            flops=flops,
            bytes_accessed=sum(array.size * array.dtype.itemsize for array in operands),
            transcendentals=0,
        ),
        name=name,
    )(*operands)
    return out[0] if len(shapes) == 1 else out


def tile(ref, index):
    return ref[:, index * HALF : (index + 1) * HALF, :].reshape(PART, 128)


def keys_of(data, name):
    if name[1] == "0":
        wide = [tile(data[name], part) for part in range(PARTS)]
    else:
        wide = [tile(data[name[0] + "0"], PARTS + part) for part in range(EARLY)]
        wide += [tile(data[name], part) for part in range(PARTS - EARLY)]
    return jnp.concatenate(wide, axis=1)


def rank_weights(shape, axis, start):
    place = iota(shape, axis) - start
    weights = jnp.where(place == 0, 16384.0, jnp.where(place == 1, 128.0, 1.0))
    return jnp.where((place >= 0) & (place < 3), weights, 0.0).astype(jnp.bfloat16)


def cut_kernel(home_ref, body_ref, ranks_ref):
    body_ref[...] = home_ref[:, : D // 8 - EARLY * HALF, :]
    ranks_ref[...] = home_ref[:, D // 8 - EARLY * HALF :, :]


def homeward(best):
    stacked = jnp.concatenate(best, axis=0)
    widen = bits(iota((8, 128), 1) // HALF == iota((8, 128), 0))
    own_lane = iota((PART, 128), 1) % HALF == iota((PART, 128), 0) % HALF
    gather = bits(iota((GROUPS, PART), 1) // HALF == iota((GROUPS, PART), 0))
    total = jnp.zeros((GROUPS, 128), jnp.float32)
    for part in three_parts(stacked):
        lanes = jnp.where(own_lane, dot(part, widen, TN), 0.0).astype(jnp.bfloat16)
        total += dot(gather, lanes, NN)
    return total


def score_kernel(names, pairs, last, *refs):
    data = dict(zip(names, refs))
    ranks = tile(refs[len(names)], 0)
    refs = refs[len(names) + 1 :]
    if pairs is FIRST:
        carried, (out_ref, *kept) = None, refs
        for name, ref in zip(KEPT, kept):
            ref[...] = data[name][...]
    else:
        carried, out_ref = refs
    used = sorted({name for pair in pairs for name in pair[:2]})
    keys = {name: keys_of(data, name) for name in used}
    by_row, by_lane = {}, {}
    for name in used:
        start = 3 * FINALS.index(name)
        by_row[name] = dot(ranks, rank_weights((128, 128), 0, start), NN)
        by_lane[name] = dot(rank_weights((8, 128), 1, start), ranks, NT)[0:1]
    best_row, best_lane = {}, {}
    for rows, columns, forward, backward in pairs:
        scores = dot(keys[rows], keys[columns], NT)
        row_rank = jnp.concatenate([by_row[rows]] * 4, axis=1)
        lane_rank = by_lane[columns]
        if forward:
            kept = jnp.where(lane_rank < row_rank, scores, -1.0)
            folded = functools.reduce(
                jnp.maximum, [kept[:, 128 * i : 128 * (i + 1)] for i in range(4)]
            )
            best_row[rows] = jnp.maximum(best_row[rows], folded) if rows in best_row else folded
        if backward:
            kept = jnp.where(row_rank < lane_rank, scores, -1.0)
            folded = jnp.max(kept, axis=0, keepdims=True)
            if columns in best_lane:
                folded = jnp.maximum(best_lane[columns], folded)
            best_lane[columns] = folded
    best = []
    for index, name in enumerate(FINALS):
        value = jnp.full((1, PART), -1.0) if carried is None else carried[index : index + 1, :]
        if name in best_lane:
            value = jnp.maximum(value, best_lane[name])
        if name in best_row:
            value = jnp.maximum(value, jnp.max(best_row[name].T, axis=0, keepdims=True))
        best.append(value)
    if last:
        out_ref[...] = homeward(best).reshape(GROUPS, 1, 128)
    else:
        out_ref[...] = jnp.concatenate(best, axis=0)


def score(blocks, pairs, carried, last, name):
    used = {half for pair in pairs for half in pair[:2]}
    names = tuple(sorted(used | {half[0] + "0" for half in used if EARLY}))
    shape = ((GROUPS, 1, 128) if last else (8, PART), jnp.float32)
    shapes = [shape]
    if pairs is FIRST:
        shapes += [(blocks[half].shape, blocks[half].dtype) for half in KEPT]
    operands = [blocks[half] for half in names + ("ranks",)] + ([] if carried is None else [carried])
    return call(
        functools.partial(score_kernel, names, pairs, last),
        name,
        shapes,
        *operands,
        flops=2 * len(pairs) * PART * PART * D,
    )


FIRST = (
    ("o0", "o0", True, False),
    ("o0", "s0", True, False),
    ("o0", "b0", True, True),
    ("s0", "b0", True, True),
    ("z0", "b0", True, True),
)
SECOND = (
    ("o1", "o1", True, False),
    ("o0", "o1", True, True),
    ("o1", "b0", True, True),
    ("o1", "s1", True, False),
    ("o0", "s1", True, True),
    ("s1", "b0", True, True),
    ("o1", "z0", True, True),
    ("s1", "z0", True, True),
)
THIRD = (
    ("o1", "b1", True, True),
    ("s1", "b1", True, True),
    ("z0", "b1", True, True),
    ("z1", "b0", True, True),
    ("z1", "b1", True, True),
)


def finish_kernel(own_ref, swap_ref, next_ref, last_ref, pos_ref, out_ref):
    block = iota((GROUPS, 128), 1) // SLOTS
    mine = last_ref[...].reshape(GROUPS, 128)
    for index, ref in enumerate((own_ref, swap_ref, next_ref)):
        mine = jnp.where(block == index, ref[...].reshape(GROUPS, 128), mine)
    position = pos_ref[...]
    member = bits(iota((GROUPS, ROWS), 0) == position // SLOTS)
    found = jnp.zeros((128, ROWS), jnp.float32)
    for part in three_parts(mine):
        found += dot(part, member, TN)
    best = functools.reduce(
        jnp.maximum, [found[SLOTS * index : SLOTS * (index + 1)] for index in range(4)]
    )
    here = iota((SLOTS, ROWS), 0) == (position & (SLOTS - 1))
    out_ref[...] = jnp.sum(jnp.where(here, best, 0.0), axis=0, keepdims=True)


FROM_NEXT = [
    (((x + 1) % 4) * 2 + (c if x < 2 else 1 - c), x * 2 + c) for x in range(4) for c in range(2)
]
FROM_LAST = [(((x - 1) % 4) * 2 + c, x * 2 + c) for x in range(4) for c in range(2)]
SWAP = [(x * 2 + 1 - c, x * 2 + c) for x in range(4) for c in range(2)]


def back(pairs):
    return [(there, here) for here, there in pairs]


def send(array, pairs):
    return lax.ppermute(array, ("x", "c"), pairs)


def spread(array):
    return send(array, SWAP), send(array, FROM_NEXT), send(array, FROM_LAST)


def to_home(array):
    return lax.all_to_all(array, ("y", "z"), split_axis=0, concat_axis=0, tiled=True)


def on_device(embeddings, cluster_ids, ranks):
    bf16 = jnp.bfloat16
    first, table, unit, position = call(
        pack_first,
        "pack_first",
        [
            ((GROUPS, D // 8 + EARLY * HALF, 128), bf16),
            ((GROUPS, HALF, 128), bf16),
            ((ROWS, D), bf16),
            ((1, ROWS), jnp.int32),
        ],
        embeddings,
        cluster_ids.reshape(1, ROWS),
        ranks.reshape(1, ROWS),
        flops=2 * PART * ROWS * D,
        scratch=[
            pltpu.VMEM((ROWS, D), jnp.float32),
            pltpu.VMEM((1, ROWS), jnp.int32),
            pltpu.VMEM((1, ROWS), jnp.int32),
            pltpu.SemaphoreType.DMA((CUTS + 2,)),
        ],
        limit=60 * 1024 * 1024,
    )
    second = call(
        pack_second,
        "pack_second",
        [((GROUPS, D // 8 + (1 - EARLY) * HALF, 128), bf16)],
        unit,
        position,
        table,
        *spread(table),
        flops=2 * PART * ROWS * D,
    )
    blocks = {}
    home = to_home(first)
    for half in "01":
        if half == "1":
            home, blocks["ranks"] = call(
                cut_kernel,
                "cut",
                [((GROUPS, D // 8 - EARLY * HALF, 128), bf16), ((GROUPS, HALF, 128), bf16)],
                to_home(second),
            )
        blocks["o" + half] = home
        for block, moved in zip("sbz", spread(home)):
            blocks[block + half] = moved
    best, *kept = score(blocks, FIRST, None, False, "score_first")
    blocks.update(zip(KEPT, kept))
    best = score(blocks, SECOND, best, False, "score_second")
    own = to_home(score(blocks, THIRD, best, True, "score_third"))
    nearest = call(
        finish_kernel,
        "finish",
        [((1, ROWS), jnp.float32)],
        own,
        send(own, back(SWAP)),
        send(own, back(FROM_NEXT)),
        send(own, back(FROM_LAST)),
        position,
    )
    return nearest.reshape(ROWS)


def solution(mesh):
    fine = Mesh(mesh.devices.reshape(tuple(SIZE.values())), tuple(SIZE))
    rows = P(tuple(SIZE))
    return jax.shard_map(
        on_device,
        mesh=fine,
        in_specs=(P(tuple(SIZE), None), P(tuple(SIZE), None), rows),
        out_specs=rows,
        check_vma=False,
    )
```

```python
import functools

import jax
import jax.numpy as jnp
from jax import lax
from jax.experimental import pallas as pl
from jax.experimental.pallas import tpu as pltpu
from jax.sharding import Mesh, PartitionSpec as P

D = 768
ROWS = 512
GROUPS = 32
HALF = 16
SLOTS = 2 * HALF
PART = GROUPS * HALF
PARTS = D // 128
SIZE = {"x": 4, "y": 4, "c": 2, "z": 8}
EARLY = 1
CUTS = 4
LIMIT = 24 * 1024 * 1024
NT = (((1,), (1,)), ((), ()))
NN = (((1,), (0,)), ((), ()))
TN = (((0,), (0,)), ((), ()))
BLOCKS = ("o", "s", "b", "z")
KEPT = ("b0", "z0")
FINALS = tuple(block + half for block in BLOCKS for half in "01")


def dot(a, b, dims):
    return lax.dot_general(a, b, dims, preferred_element_type=jnp.float32)


def iota(shape, axis):
    return lax.broadcasted_iota(jnp.int32, shape, axis)


def bits(mask):
    return mask.astype(jnp.float32).astype(jnp.bfloat16)


def three_parts(value):
    parts = []
    for _ in range(3):
        part = value.astype(jnp.bfloat16)
        parts.append(part)
        value = value - part.astype(jnp.float32)
    return parts


def chosen_rows(position, half):
    slot, group = position & (SLOTS - 1), position // SLOTS
    row = jnp.where(slot // HALF == half, group * HALF + slot % HALF, -1)
    return bits(iota((PART, ROWS), 0) == row)


def put(moved, out_ref, start):
    moved = moved.astype(jnp.bfloat16)
    for part in range(moved.shape[1] // 128):
        rows = start + part * HALF
        out_ref[:, rows : rows + HALF, :] = moved[:, part * 128 : (part + 1) * 128].reshape(
            GROUPS, HALF, 128
        )


def pack_first(
    emb_hbm, ids_hbm, rank_hbm, out_ref, table_ref, unit_ref, pos_ref, emb_ref, ids_ref, rank_ref, sems
):
    pieces = [pl.ds(start, ROWS // CUTS) for start in range(0, ROWS, ROWS // CUTS)]
    copies = [
        pltpu.make_async_copy(ids_hbm, ids_ref, sems.at[CUTS]),
        pltpu.make_async_copy(rank_hbm, rank_ref, sems.at[CUTS + 1]),
    ] + [
        pltpu.make_async_copy(emb_hbm.at[piece], emb_ref.at[piece], sems.at[index])
        for index, piece in enumerate(pieces)
    ]
    for copy in copies:
        copy.start()
    for copy in copies[:2]:
        copy.wait()

    target = ids_ref[...]
    member = (iota((GROUPS, ROWS), 0) == target).astype(jnp.float32)
    earlier = bits(iota((ROWS, ROWS), 0) < iota((ROWS, ROWS), 1))
    before = dot(member.astype(jnp.bfloat16), earlier, NN)
    slot = jnp.sum(before * member, axis=0, keepdims=True).astype(jnp.int32)
    position = target * SLOTS + slot
    pos_ref[...] = position

    first, second = chosen_rows(position, 0), chosen_rows(position, 1)
    for copy, piece in zip(copies[2:], pieces):
        copy.wait()
        rows = emb_ref[piece, :]
        norms = jnp.sum(rows * rows, axis=1, keepdims=True)
        unit_ref[piece, :] = (rows * lax.rsqrt(norms + 1e-06)).astype(jnp.bfloat16)
    unit = unit_ref[...]
    put(dot(first, unit, NN), out_ref, 0)
    if EARLY:
        put(dot(second, unit[:, : EARLY * 128], NN), out_ref, D // 8)
    rank = rank_ref[...]
    line = iota((128, ROWS), 0)
    ranks = jnp.zeros((PART, 128), jnp.float32)
    for half, chosen in enumerate((first, second)):
        parts = jnp.zeros((128, ROWS), jnp.int32)
        for index, part in enumerate(((rank >> 14) - 128, (rank >> 7) & 127, rank & 127)):
            parts = jnp.where(line == 3 * half + index, part, parts)
        ranks += dot(chosen, parts.astype(jnp.float32).astype(jnp.bfloat16), NT)
    put(ranks, table_ref, 0)


def pack_second(unit_ref, pos_ref, *refs):
    out_ref = refs[-1]
    put(dot(chosen_rows(pos_ref[...], 1), unit_ref[:, EARLY * 128 :], NN), out_ref, 0)
    ranks = jnp.zeros((PART, 128), jnp.float32)
    lane, other = iota((128, 128), 0), iota((128, 128), 1)
    for index, table_ref in enumerate(refs[:-1]):
        moved = bits((lane < 6) & (other == lane + 6 * index))
        ranks += dot(tile(table_ref, 0), moved, NN)
    put(ranks, out_ref, D // 8 - EARLY * HALF)


def vmem(count):
    return [pl.BlockSpec(memory_space=pltpu.VMEM)] * count


def call(kernel, name, shapes, *operands, flops=0, scratch=None, limit=LIMIT):
    shapes = tuple(jax.ShapeDtypeStruct(shape, dtype) for shape, dtype in shapes)
    out = pl.pallas_call(
        kernel,
        out_shape=shapes,
        in_specs=[pl.BlockSpec(memory_space=pltpu.HBM)] * len(operands) if scratch else vmem(len(operands)),
        out_specs=tuple(vmem(len(shapes))),
        scratch_shapes=scratch or [],
        compiler_params=pltpu.CompilerParams(vmem_limit_bytes=limit),
        cost_estimate=pl.CostEstimate(
            flops=flops,
            bytes_accessed=sum(array.size * array.dtype.itemsize for array in operands),
            transcendentals=0,
        ),
        name=name,
    )(*operands)
    return out[0] if len(shapes) == 1 else out


def tile(ref, index):
    return ref[:, index * HALF : (index + 1) * HALF, :].reshape(PART, 128)


def keys_of(data, name):
    if name[1] == "0":
        wide = [tile(data[name], part) for part in range(PARTS)]
    else:
        wide = [tile(data[name[0] + "0"], PARTS + part) for part in range(EARLY)]
        wide += [tile(data[name], part) for part in range(PARTS - EARLY)]
    return jnp.concatenate(wide, axis=1)


def rank_weights(shape, axis, start):
    place = iota(shape, axis) - start
    weights = jnp.where(place == 0, 16384.0, jnp.where(place == 1, 128.0, 1.0))
    return jnp.where((place >= 0) & (place < 3), weights, 0.0).astype(jnp.bfloat16)


def cut_kernel(home_ref, body_ref, ranks_ref):
    body_ref[...] = home_ref[:, : D // 8 - EARLY * HALF, :]
    ranks_ref[...] = home_ref[:, D // 8 - EARLY * HALF :, :]


def homeward(best):
    stacked = jnp.concatenate(best, axis=0)
    widen = bits(iota((8, 128), 1) // HALF == iota((8, 128), 0))
    own_lane = iota((PART, 128), 1) % HALF == iota((PART, 128), 0) % HALF
    gather = bits(iota((GROUPS, PART), 1) // HALF == iota((GROUPS, PART), 0))
    total = jnp.zeros((GROUPS, 128), jnp.float32)
    for part in three_parts(stacked):
        lanes = jnp.where(own_lane, dot(part, widen, TN), 0.0).astype(jnp.bfloat16)
        total += dot(gather, lanes, NN)
    return total


def score_kernel(names, pairs, last, *refs):
    data = dict(zip(names, refs))
    ranks = tile(refs[len(names)], 0)
    refs = refs[len(names) + 1 :]
    if pairs is FIRST:
        carried, (out_ref, *kept) = None, refs
        for name, ref in zip(KEPT, kept):
            ref[...] = data[name][...]
    else:
        carried, out_ref = refs
    used = sorted({name for pair in pairs for name in pair[:2]})
    keys = {name: keys_of(data, name) for name in used}
    by_row, by_lane = {}, {}
    for name in used:
        start = 3 * FINALS.index(name)
        by_row[name] = dot(ranks, rank_weights((128, 128), 0, start), NN)
        by_lane[name] = dot(rank_weights((8, 128), 1, start), ranks, NT)[0:1]
    best_row, best_lane = {}, {}
    for rows, columns, forward, backward in pairs:
        scores = dot(keys[rows], keys[columns], NT)
        row_rank = jnp.concatenate([by_row[rows]] * 4, axis=1)
        lane_rank = by_lane[columns]
        if forward:
            kept = jnp.where(lane_rank < row_rank, scores, -1.0)
            folded = functools.reduce(
                jnp.maximum, [kept[:, 128 * i : 128 * (i + 1)] for i in range(4)]
            )
            best_row[rows] = jnp.maximum(best_row[rows], folded) if rows in best_row else folded
        if backward:
            kept = jnp.where(row_rank < lane_rank, scores, -1.0)
            folded = jnp.max(kept, axis=0, keepdims=True)
            if columns in best_lane:
                folded = jnp.maximum(best_lane[columns], folded)
            best_lane[columns] = folded
    best = []
    for index, name in enumerate(FINALS):
        value = jnp.full((1, PART), -1.0) if carried is None else carried[index : index + 1, :]
        if name in best_lane:
            value = jnp.maximum(value, best_lane[name])
        if name in best_row:
            value = jnp.maximum(value, jnp.max(best_row[name].T, axis=0, keepdims=True))
        best.append(value)
    if last:
        out_ref[...] = homeward(best).reshape(GROUPS, 1, 128)
    else:
        out_ref[...] = jnp.concatenate(best, axis=0)


def score(blocks, pairs, carried, last, name):
    used = {half for pair in pairs for half in pair[:2]}
    names = tuple(sorted(used | {half[0] + "0" for half in used if EARLY}))
    shape = ((GROUPS, 1, 128) if last else (8, PART), jnp.float32)
    shapes = [shape]
    if pairs is FIRST:
        shapes += [(blocks[half].shape, blocks[half].dtype) for half in KEPT]
    operands = [blocks[half] for half in names + ("ranks",)] + ([] if carried is None else [carried])
    return call(
        functools.partial(score_kernel, names, pairs, last),
        name,
        shapes,
        *operands,
        flops=2 * len(pairs) * PART * PART * D,
    )


FIRST = (
    ("o0", "o0", True, False),
    ("o0", "s0", True, False),
    ("o0", "b0", True, True),
    ("s0", "b0", True, True),
    ("z0", "b0", True, True),
)
SECOND = (
    ("o1", "o1", True, False),
    ("o0", "o1", True, True),
    ("o1", "b0", True, True),
    ("o1", "s1", True, False),
    ("o0", "s1", True, True),
    ("s1", "b0", True, True),
    ("o1", "z0", True, True),
    ("s1", "z0", True, True),
)
THIRD = (
    ("o1", "b1", True, True),
    ("s1", "b1", True, True),
    ("z0", "b1", True, True),
)
FOURTH = (
    ("z1", "b0", True, True),
    ("z1", "b1", True, True),
)


def finish_kernel(own_ref, swap_ref, next_ref, last_ref, pos_ref, out_ref):
    block = iota((GROUPS, 128), 1) // SLOTS
    mine = last_ref[...].reshape(GROUPS, 128)
    for index, ref in enumerate((own_ref, swap_ref, next_ref)):
        mine = jnp.where(block == index, ref[...].reshape(GROUPS, 128), mine)
    position = pos_ref[...]
    member = bits(iota((GROUPS, ROWS), 0) == position // SLOTS)
    found = jnp.zeros((128, ROWS), jnp.float32)
    for part in three_parts(mine):
        found += dot(part, member, TN)
    best = functools.reduce(
        jnp.maximum, [found[SLOTS * index : SLOTS * (index + 1)] for index in range(4)]
    )
    here = iota((SLOTS, ROWS), 0) == (position & (SLOTS - 1))
    out_ref[...] = jnp.sum(jnp.where(here, best, 0.0), axis=0, keepdims=True)


FROM_NEXT = [
    (((x + 1) % 4) * 2 + (c if x < 2 else 1 - c), x * 2 + c) for x in range(4) for c in range(2)
]
FROM_LAST = [(((x - 1) % 4) * 2 + c, x * 2 + c) for x in range(4) for c in range(2)]
SWAP = [(x * 2 + 1 - c, x * 2 + c) for x in range(4) for c in range(2)]


def back(pairs):
    return [(there, here) for here, there in pairs]


def send(array, pairs):
    return lax.ppermute(array, ("x", "c"), pairs)


def spread(array):
    return send(array, SWAP), send(array, FROM_NEXT), send(array, FROM_LAST)


def to_home(array):
    return lax.all_to_all(array, ("y", "z"), split_axis=0, concat_axis=0, tiled=True)


def on_device(embeddings, cluster_ids, ranks):
    bf16 = jnp.bfloat16
    first, table, unit, position = call(
        pack_first,
        "pack_first",
        [
            ((GROUPS, D // 8 + EARLY * HALF, 128), bf16),
            ((GROUPS, HALF, 128), bf16),
            ((ROWS, D), bf16),
            ((1, ROWS), jnp.int32),
        ],
        embeddings,
        cluster_ids.reshape(1, ROWS),
        ranks.reshape(1, ROWS),
        flops=2 * PART * ROWS * D,
        scratch=[
            pltpu.VMEM((ROWS, D), jnp.float32),
            pltpu.VMEM((1, ROWS), jnp.int32),
            pltpu.VMEM((1, ROWS), jnp.int32),
            pltpu.SemaphoreType.DMA((CUTS + 2,)),
        ],
        limit=60 * 1024 * 1024,
    )
    second = call(
        pack_second,
        "pack_second",
        [((GROUPS, D // 8 + (1 - EARLY) * HALF, 128), bf16)],
        unit,
        position,
        table,
        *spread(table),
        flops=2 * PART * ROWS * D,
    )
    blocks = {}
    home = to_home(first)
    for half in "01":
        if half == "1":
            home, blocks["ranks"] = call(
                cut_kernel,
                "cut",
                [((GROUPS, D // 8 - EARLY * HALF, 128), bf16), ((GROUPS, HALF, 128), bf16)],
                to_home(second),
            )
        blocks["o" + half] = home
        for block, moved in zip("sbz", spread(home)):
            blocks[block + half] = moved
    best, *kept = score(blocks, FIRST, None, False, "score_first")
    blocks.update(zip(KEPT, kept))
    best = score(blocks, SECOND, best, False, "score_second")
    best = score(blocks, THIRD, best, False, "score_third")
    own = to_home(score(blocks, FOURTH, best, True, "score_fourth"))
    nearest = call(
        finish_kernel,
        "finish",
        [((1, ROWS), jnp.float32)],
        own,
        send(own, back(SWAP)),
        send(own, back(FROM_NEXT)),
        send(own, back(FROM_LAST)),
        position,
    )
    return nearest.reshape(ROWS)


def solution(mesh):
    fine = Mesh(mesh.devices.reshape(tuple(SIZE.values())), tuple(SIZE))
    rows = P(tuple(SIZE))
    return jax.shard_map(
        on_device,
        mesh=fine,
        in_specs=(P(tuple(SIZE), None), P(tuple(SIZE), None), rows),
        out_specs=rows,
        check_vma=False,
    )
```

```python
import functools

import jax
import jax.numpy as jnp
from jax import lax
from jax.experimental import pallas as pl
from jax.experimental.pallas import tpu as pltpu
from jax.sharding import Mesh, PartitionSpec as P

D = 768
ROWS = 512
GROUPS = 32
HALF = 16
SLOTS = 2 * HALF
PART = GROUPS * HALF
PARTS = D // 128
SIZE = {"x": 4, "y": 4, "c": 2, "z": 8}
EARLY = 1
CUTS = 4
LIMIT = 24 * 1024 * 1024
NT = (((1,), (1,)), ((), ()))
NN = (((1,), (0,)), ((), ()))
TN = (((0,), (0,)), ((), ()))
BLOCKS = ("o", "s", "b", "z")
KEPT = ("b0", "z0")
FINALS = tuple(block + half for block in BLOCKS for half in "01")


def dot(a, b, dims):
    return lax.dot_general(a, b, dims, preferred_element_type=jnp.float32)


def iota(shape, axis):
    return lax.broadcasted_iota(jnp.int32, shape, axis)


def bits(mask):
    return mask.astype(jnp.float32).astype(jnp.bfloat16)


def three_parts(value):
    parts = []
    for _ in range(3):
        part = value.astype(jnp.bfloat16)
        parts.append(part)
        value = value - part.astype(jnp.float32)
    return parts


def chosen_rows(position, half):
    slot, group = position & (SLOTS - 1), position // SLOTS
    row = jnp.where(slot // HALF == half, group * HALF + slot % HALF, -1)
    return bits(iota((PART, ROWS), 0) == row)


def put(moved, out_ref, start):
    moved = moved.astype(jnp.bfloat16)
    for part in range(moved.shape[1] // 128):
        rows = start + part * HALF
        out_ref[:, rows : rows + HALF, :] = moved[:, part * 128 : (part + 1) * 128].reshape(
            GROUPS, HALF, 128
        )


def normalise(rows):
    norms = jnp.sum(rows * rows, axis=1, keepdims=True)
    return (rows * lax.rsqrt(norms + 1e-06)).astype(jnp.bfloat16)


def pack_first(emb_hbm, ids_hbm, out_ref, pos_ref, emb_ref, ids_ref, unit_ref, sems):
    pieces = [pl.ds(start, ROWS // CUTS) for start in range(0, ROWS, ROWS // CUTS)]
    small = pltpu.make_async_copy(ids_hbm, ids_ref, sems.at[CUTS])
    copies = [
        pltpu.make_async_copy(emb_hbm.at[piece], emb_ref.at[piece], sems.at[index])
        for index, piece in enumerate(pieces)
    ]
    for copy in [small, *copies]:
        copy.start()
    small.wait()

    target = ids_ref[...]
    member = (iota((GROUPS, ROWS), 0) == target).astype(jnp.float32)
    earlier = bits(iota((ROWS, ROWS), 0) < iota((ROWS, ROWS), 1))
    before = dot(member.astype(jnp.bfloat16), earlier, NN)
    slot = jnp.sum(before * member, axis=0, keepdims=True).astype(jnp.int32)
    position = target * SLOTS + slot
    pos_ref[...] = position

    first, second = chosen_rows(position, 0), chosen_rows(position, 1)
    for copy, piece in zip(copies, pieces):
        copy.wait()
        unit_ref[piece, :] = normalise(emb_ref[piece, :])
    unit = unit_ref[...]
    put(dot(first, unit, NN), out_ref, 0)
    if EARLY:
        put(dot(second, unit[:, : EARLY * 128], NN), out_ref, D // 8)


def pack_table(pos_ref, rank_ref, table_ref):
    rank = rank_ref[...]
    line = iota((128, ROWS), 0)
    ranks = jnp.zeros((PART, 128), jnp.float32)
    for half in range(2):
        parts = jnp.zeros((128, ROWS), jnp.int32)
        for index, part in enumerate(((rank >> 14) - 128, (rank >> 7) & 127, rank & 127)):
            parts = jnp.where(line == 3 * half + index, part, parts)
        chosen = chosen_rows(pos_ref[...], half)
        ranks += dot(chosen, parts.astype(jnp.float32).astype(jnp.bfloat16), NT)
    put(ranks, table_ref, 0)


def pack_second(emb_ref, pos_ref, *refs):
    out_ref = refs[-1]
    unit = normalise(emb_ref[...])
    put(dot(chosen_rows(pos_ref[...], 1), unit[:, EARLY * 128 :], NN), out_ref, 0)
    ranks = jnp.zeros((PART, 128), jnp.float32)
    lane, other = iota((128, 128), 0), iota((128, 128), 1)
    for index, table_ref in enumerate(refs[:-1]):
        moved = bits((lane < 6) & (other == lane + 6 * index))
        ranks += dot(tile(table_ref, 0), moved, NN)
    put(ranks, out_ref, D // 8 - EARLY * HALF)


def vmem(count):
    return [pl.BlockSpec(memory_space=pltpu.VMEM)] * count


def call(kernel, name, shapes, *operands, flops=0, scratch=None, limit=LIMIT):
    shapes = tuple(jax.ShapeDtypeStruct(shape, dtype) for shape, dtype in shapes)
    out = pl.pallas_call(
        kernel,
        out_shape=shapes,
        in_specs=[pl.BlockSpec(memory_space=pltpu.HBM)] * len(operands) if scratch else vmem(len(operands)),
        out_specs=tuple(vmem(len(shapes))),
        scratch_shapes=scratch or [],
        compiler_params=pltpu.CompilerParams(vmem_limit_bytes=limit),
        cost_estimate=pl.CostEstimate(
            flops=flops,
            bytes_accessed=sum(array.size * array.dtype.itemsize for array in operands),
            transcendentals=0,
        ),
        name=name,
    )(*operands)
    return out[0] if len(shapes) == 1 else out


def tile(ref, index):
    return ref[:, index * HALF : (index + 1) * HALF, :].reshape(PART, 128)


def keys_of(data, name):
    if name[1] == "0":
        wide = [tile(data[name], part) for part in range(PARTS)]
    else:
        wide = [tile(data[name[0] + "0"], PARTS + part) for part in range(EARLY)]
        wide += [tile(data[name], part) for part in range(PARTS - EARLY)]
    return jnp.concatenate(wide, axis=1)


def rank_weights(shape, axis, start):
    place = iota(shape, axis) - start
    weights = jnp.where(place == 0, 16384.0, jnp.where(place == 1, 128.0, 1.0))
    return jnp.where((place >= 0) & (place < 3), weights, 0.0).astype(jnp.bfloat16)


def cut_kernel(home_ref, body_ref, ranks_ref):
    body_ref[...] = home_ref[:, : D // 8 - EARLY * HALF, :]
    ranks_ref[...] = home_ref[:, D // 8 - EARLY * HALF :, :]


def homeward(best):
    stacked = jnp.concatenate(best, axis=0)
    widen = bits(iota((8, 128), 1) // HALF == iota((8, 128), 0))
    own_lane = iota((PART, 128), 1) % HALF == iota((PART, 128), 0) % HALF
    gather = bits(iota((GROUPS, PART), 1) // HALF == iota((GROUPS, PART), 0))
    total = jnp.zeros((GROUPS, 128), jnp.float32)
    for part in three_parts(stacked):
        lanes = jnp.where(own_lane, dot(part, widen, TN), 0.0).astype(jnp.bfloat16)
        total += dot(gather, lanes, NN)
    return total


def score_kernel(names, pairs, last, *refs):
    data = dict(zip(names, refs))
    ranks = tile(refs[len(names)], 0)
    refs = refs[len(names) + 1 :]
    if pairs is FIRST:
        carried, (out_ref, *kept) = None, refs
        for name, ref in zip(KEPT, kept):
            ref[...] = data[name][...]
    else:
        carried, out_ref = refs
    used = sorted({name for pair in pairs for name in pair[:2]})
    keys = {name: keys_of(data, name) for name in used}
    by_row, by_lane = {}, {}
    for name in used:
        start = 3 * FINALS.index(name)
        by_row[name] = dot(ranks, rank_weights((128, 128), 0, start), NN)
        by_lane[name] = dot(rank_weights((8, 128), 1, start), ranks, NT)[0:1]
    best_row, best_lane = {}, {}
    for rows, columns, forward, backward in pairs:
        scores = dot(keys[rows], keys[columns], NT)
        row_rank = jnp.concatenate([by_row[rows]] * 4, axis=1)
        lane_rank = by_lane[columns]
        if forward:
            kept = jnp.where(lane_rank < row_rank, scores, -1.0)
            folded = functools.reduce(
                jnp.maximum, [kept[:, 128 * i : 128 * (i + 1)] for i in range(4)]
            )
            best_row[rows] = jnp.maximum(best_row[rows], folded) if rows in best_row else folded
        if backward:
            kept = jnp.where(row_rank < lane_rank, scores, -1.0)
            folded = jnp.max(kept, axis=0, keepdims=True)
            if columns in best_lane:
                folded = jnp.maximum(best_lane[columns], folded)
            best_lane[columns] = folded
    best = []
    for index, name in enumerate(FINALS):
        value = jnp.full((1, PART), -1.0) if carried is None else carried[index : index + 1, :]
        if name in best_lane:
            value = jnp.maximum(value, best_lane[name])
        if name in best_row:
            value = jnp.maximum(value, jnp.max(best_row[name].T, axis=0, keepdims=True))
        best.append(value)
    if last:
        out_ref[...] = homeward(best).reshape(GROUPS, 1, 128)
    else:
        out_ref[...] = jnp.concatenate(best, axis=0)


def score(blocks, pairs, carried, last, name):
    used = {half for pair in pairs for half in pair[:2]}
    names = tuple(sorted(used | {half[0] + "0" for half in used if EARLY}))
    shape = ((GROUPS, 1, 128) if last else (8, PART), jnp.float32)
    shapes = [shape]
    if pairs is FIRST:
        shapes += [(blocks[half].shape, blocks[half].dtype) for half in KEPT]
    operands = [blocks[half] for half in names + ("ranks",)] + ([] if carried is None else [carried])
    return call(
        functools.partial(score_kernel, names, pairs, last),
        name,
        shapes,
        *operands,
        flops=2 * len(pairs) * PART * PART * D,
    )


FIRST = (
    ("o0", "o0", True, False),
    ("o0", "s0", True, False),
    ("o0", "b0", True, True),
    ("s0", "b0", True, True),
    ("z0", "b0", True, True),
)
SECOND = (
    ("o1", "o1", True, False),
    ("o0", "o1", True, True),
    ("o1", "b0", True, True),
    ("o1", "s1", True, False),
    ("o0", "s1", True, True),
    ("s1", "b0", True, True),
    ("o1", "z0", True, True),
    ("s1", "z0", True, True),
)
THIRD = (
    ("o1", "b1", True, True),
    ("s1", "b1", True, True),
    ("z0", "b1", True, True),
)
FOURTH = (
    ("z1", "b0", True, True),
    ("z1", "b1", True, True),
)


def finish_kernel(own_ref, swap_ref, next_ref, last_ref, pos_ref, out_ref):
    block = iota((GROUPS, 128), 1) // SLOTS
    mine = last_ref[...].reshape(GROUPS, 128)
    for index, ref in enumerate((own_ref, swap_ref, next_ref)):
        mine = jnp.where(block == index, ref[...].reshape(GROUPS, 128), mine)
    position = pos_ref[...]
    member = bits(iota((GROUPS, ROWS), 0) == position // SLOTS)
    found = jnp.zeros((128, ROWS), jnp.float32)
    for part in three_parts(mine):
        found += dot(part, member, TN)
    best = functools.reduce(
        jnp.maximum, [found[SLOTS * index : SLOTS * (index + 1)] for index in range(4)]
    )
    here = iota((SLOTS, ROWS), 0) == (position & (SLOTS - 1))
    out_ref[...] = jnp.sum(jnp.where(here, best, 0.0), axis=0, keepdims=True)


FROM_NEXT = [
    (((x + 1) % 4) * 2 + (c if x < 2 else 1 - c), x * 2 + c) for x in range(4) for c in range(2)
]
FROM_LAST = [(((x - 1) % 4) * 2 + c, x * 2 + c) for x in range(4) for c in range(2)]
SWAP = [(x * 2 + 1 - c, x * 2 + c) for x in range(4) for c in range(2)]


def back(pairs):
    return [(there, here) for here, there in pairs]


def send(array, pairs):
    return lax.ppermute(array, ("x", "c"), pairs)


def spread(array):
    return send(array, SWAP), send(array, FROM_NEXT), send(array, FROM_LAST)


def to_home(array):
    return lax.all_to_all(array, ("y", "z"), split_axis=0, concat_axis=0, tiled=True)


def on_device(embeddings, cluster_ids, ranks):
    bf16 = jnp.bfloat16
    first, position = call(
        pack_first,
        "pack_first",
        [((GROUPS, D // 8 + EARLY * HALF, 128), bf16), ((1, ROWS), jnp.int32)],
        embeddings,
        cluster_ids.reshape(1, ROWS),
        flops=2 * PART * ROWS * D,
        scratch=[
            pltpu.VMEM((ROWS, D), jnp.float32),
            pltpu.VMEM((1, ROWS), jnp.int32),
            pltpu.VMEM((ROWS, D), bf16),
            pltpu.SemaphoreType.DMA((CUTS + 1,)),
        ],
        limit=60 * 1024 * 1024,
    )
    table = call(
        pack_table,
        "pack_table",
        [((GROUPS, HALF, 128), bf16)],
        position,
        ranks.reshape(1, ROWS),
    )
    second = call(
        pack_second,
        "pack_second",
        [((GROUPS, D // 8 + (1 - EARLY) * HALF, 128), bf16)],
        embeddings,
        position,
        table,
        *spread(table),
        flops=2 * PART * ROWS * D,
    )
    blocks = {}
    home = to_home(first)
    for half in "01":
        if half == "1":
            home, blocks["ranks"] = call(
                cut_kernel,
                "cut",
                [((GROUPS, D // 8 - EARLY * HALF, 128), bf16), ((GROUPS, HALF, 128), bf16)],
                to_home(second),
            )
        blocks["o" + half] = home
        for block, moved in zip("sbz", spread(home)):
            blocks[block + half] = moved
    best, *kept = score(blocks, FIRST, None, False, "score_first")
    blocks.update(zip(KEPT, kept))
    best = score(blocks, SECOND, best, False, "score_second")
    best = score(blocks, THIRD, best, False, "score_third")
    own = to_home(score(blocks, FOURTH, best, True, "score_fourth"))
    nearest = call(
        finish_kernel,
        "finish",
        [((1, ROWS), jnp.float32)],
        own,
        send(own, back(SWAP)),
        send(own, back(FROM_NEXT)),
        send(own, back(FROM_LAST)),
        position,
    )
    return nearest.reshape(ROWS)


def solution(mesh):
    fine = Mesh(mesh.devices.reshape(tuple(SIZE.values())), tuple(SIZE))
    rows = P(tuple(SIZE))
    return jax.shard_map(
        on_device,
        mesh=fine,
        in_specs=(P(tuple(SIZE), None), P(tuple(SIZE), None), rows),
        out_specs=rows,
        check_vma=False,
    )
```

```python
import functools

import jax
import jax.numpy as jnp
from jax import lax
from jax.experimental import pallas as pl
from jax.experimental.pallas import tpu as pltpu
from jax.sharding import Mesh, PartitionSpec as P

D = 768
ROWS = 512
GROUPS = 32
HALF = 16
SLOTS = 2 * HALF
PART = GROUPS * HALF
PARTS = D // 128
SIZE = {"x": 4, "y": 4, "c": 2, "z": 8}
EARLY = 1
CUTS = 2
LIMIT = 24 * 1024 * 1024
NT = (((1,), (1,)), ((), ()))
NN = (((1,), (0,)), ((), ()))
TN = (((0,), (0,)), ((), ()))
BLOCKS = ("o", "s", "b", "z")
KEPT = ("b0", "z0")
FINALS = tuple(block + half for block in BLOCKS for half in "01")


def dot(a, b, dims):
    return lax.dot_general(a, b, dims, preferred_element_type=jnp.float32)


def iota(shape, axis):
    return lax.broadcasted_iota(jnp.int32, shape, axis)


def bits(mask):
    return mask.astype(jnp.float32).astype(jnp.bfloat16)


def three_parts(value):
    parts = []
    for _ in range(3):
        part = value.astype(jnp.bfloat16)
        parts.append(part)
        value = value - part.astype(jnp.float32)
    return parts


def chosen_rows(position, half):
    slot, group = position & (SLOTS - 1), position // SLOTS
    row = jnp.where(slot // HALF == half, group * HALF + slot % HALF, -1)
    return bits(iota((PART, ROWS), 0) == row)


def put(moved, out_ref, start):
    moved = moved.astype(jnp.bfloat16)
    for part in range(moved.shape[1] // 128):
        rows = start + part * HALF
        out_ref[:, rows : rows + HALF, :] = moved[:, part * 128 : (part + 1) * 128].reshape(
            GROUPS, HALF, 128
        )


def normalise(rows):
    norms = jnp.sum(rows * rows, axis=1, keepdims=True)
    return (rows * lax.rsqrt(norms + 1e-06)).astype(jnp.bfloat16)


def pack_first(emb_hbm, ids_hbm, out_ref, pos_ref, emb_ref, ids_ref, unit_ref, sems):
    pieces = [pl.ds(start, ROWS // CUTS) for start in range(0, ROWS, ROWS // CUTS)]
    small = pltpu.make_async_copy(ids_hbm, ids_ref, sems.at[CUTS])
    copies = [
        pltpu.make_async_copy(emb_hbm.at[piece], emb_ref.at[piece], sems.at[index])
        for index, piece in enumerate(pieces)
    ]
    for copy in [small, *copies]:
        copy.start()
    small.wait()

    target = ids_ref[...]
    member = (iota((GROUPS, ROWS), 0) == target).astype(jnp.float32)
    earlier = bits(iota((ROWS, ROWS), 0) < iota((ROWS, ROWS), 1))
    before = dot(member.astype(jnp.bfloat16), earlier, NN)
    slot = jnp.sum(before * member, axis=0, keepdims=True).astype(jnp.int32)
    position = target * SLOTS + slot
    pos_ref[...] = position

    first, second = chosen_rows(position, 0), chosen_rows(position, 1)
    for copy, piece in zip(copies, pieces):
        copy.wait()
        unit_ref[piece, :] = normalise(emb_ref[piece, :])
    unit = unit_ref[...]
    put(dot(first, unit, NN), out_ref, 0)
    if EARLY:
        put(dot(second, unit[:, : EARLY * 128], NN), out_ref, D // 8)


def pack_table(pos_ref, rank_ref, table_ref):
    rank = rank_ref[...]
    line = iota((128, ROWS), 0)
    ranks = jnp.zeros((PART, 128), jnp.float32)
    for half in range(2):
        parts = jnp.zeros((128, ROWS), jnp.int32)
        for index, part in enumerate(((rank >> 14) - 128, (rank >> 7) & 127, rank & 127)):
            parts = jnp.where(line == 3 * half + index, part, parts)
        chosen = chosen_rows(pos_ref[...], half)
        ranks += dot(chosen, parts.astype(jnp.float32).astype(jnp.bfloat16), NT)
    put(ranks, table_ref, 0)


def pack_second(emb_ref, pos_ref, *refs):
    out_ref = refs[-1]
    unit = normalise(emb_ref[...])
    put(dot(chosen_rows(pos_ref[...], 1), unit[:, EARLY * 128 :], NN), out_ref, 0)
    ranks = jnp.zeros((PART, 128), jnp.float32)
    lane, other = iota((128, 128), 0), iota((128, 128), 1)
    for index, table_ref in enumerate(refs[:-1]):
        moved = bits((lane < 6) & (other == lane + 6 * index))
        ranks += dot(tile(table_ref, 0), moved, NN)
    put(ranks, out_ref, D // 8 - EARLY * HALF)


def vmem(count):
    return [pl.BlockSpec(memory_space=pltpu.VMEM)] * count


def call(kernel, name, shapes, *operands, flops=0, scratch=None, limit=LIMIT):
    shapes = tuple(jax.ShapeDtypeStruct(shape, dtype) for shape, dtype in shapes)
    out = pl.pallas_call(
        kernel,
        out_shape=shapes,
        in_specs=[pl.BlockSpec(memory_space=pltpu.HBM)] * len(operands) if scratch else vmem(len(operands)),
        out_specs=tuple(vmem(len(shapes))),
        scratch_shapes=scratch or [],
        compiler_params=pltpu.CompilerParams(vmem_limit_bytes=limit),
        cost_estimate=pl.CostEstimate(
            flops=flops,
            bytes_accessed=sum(array.size * array.dtype.itemsize for array in operands),
            transcendentals=0,
        ),
        name=name,
    )(*operands)
    return out[0] if len(shapes) == 1 else out


def tile(ref, index):
    return ref[:, index * HALF : (index + 1) * HALF, :].reshape(PART, 128)


def keys_of(data, name):
    if name[1] == "0":
        wide = [tile(data[name], part) for part in range(PARTS)]
    else:
        wide = [tile(data[name[0] + "0"], PARTS + part) for part in range(EARLY)]
        wide += [tile(data[name], part) for part in range(PARTS - EARLY)]
    return jnp.concatenate(wide, axis=1)


def rank_weights(shape, axis, start):
    place = iota(shape, axis) - start
    weights = jnp.where(place == 0, 16384.0, jnp.where(place == 1, 128.0, 1.0))
    return jnp.where((place >= 0) & (place < 3), weights, 0.0).astype(jnp.bfloat16)


def cut_kernel(home_ref, body_ref, ranks_ref):
    body_ref[...] = home_ref[:, : D // 8 - EARLY * HALF, :]
    ranks_ref[...] = home_ref[:, D // 8 - EARLY * HALF :, :]


def homeward(best):
    stacked = jnp.concatenate(best, axis=0)
    widen = bits(iota((8, 128), 1) // HALF == iota((8, 128), 0))
    own_lane = iota((PART, 128), 1) % HALF == iota((PART, 128), 0) % HALF
    gather = bits(iota((GROUPS, PART), 1) // HALF == iota((GROUPS, PART), 0))
    total = jnp.zeros((GROUPS, 128), jnp.float32)
    for part in three_parts(stacked):
        lanes = jnp.where(own_lane, dot(part, widen, TN), 0.0).astype(jnp.bfloat16)
        total += dot(gather, lanes, NN)
    return total


def score_kernel(names, pairs, last, *refs):
    data = dict(zip(names, refs))
    ranks = tile(refs[len(names)], 0)
    refs = refs[len(names) + 1 :]
    if pairs is FIRST:
        carried, (out_ref, *kept) = None, refs
        for name, ref in zip(KEPT, kept):
            ref[...] = data[name][...]
    else:
        carried, out_ref = refs
    used = sorted({name for pair in pairs for name in pair[:2]})
    keys = {name: keys_of(data, name) for name in used}
    by_row, by_lane = {}, {}
    for name in used:
        start = 3 * FINALS.index(name)
        by_row[name] = dot(ranks, rank_weights((128, 128), 0, start), NN)
        by_lane[name] = dot(rank_weights((8, 128), 1, start), ranks, NT)[0:1]
    best_row, best_lane = {}, {}
    for rows, columns, forward, backward in pairs:
        scores = dot(keys[rows], keys[columns], NT)
        row_rank = jnp.concatenate([by_row[rows]] * 4, axis=1)
        lane_rank = by_lane[columns]
        if forward:
            kept = jnp.where(lane_rank < row_rank, scores, -1.0)
            folded = functools.reduce(
                jnp.maximum, [kept[:, 128 * i : 128 * (i + 1)] for i in range(4)]
            )
            best_row[rows] = jnp.maximum(best_row[rows], folded) if rows in best_row else folded
        if backward:
            kept = jnp.where(row_rank < lane_rank, scores, -1.0)
            folded = jnp.max(kept, axis=0, keepdims=True)
            if columns in best_lane:
                folded = jnp.maximum(best_lane[columns], folded)
            best_lane[columns] = folded
    best = []
    for index, name in enumerate(FINALS):
        value = jnp.full((1, PART), -1.0) if carried is None else carried[index : index + 1, :]
        if name in best_lane:
            value = jnp.maximum(value, best_lane[name])
        if name in best_row:
            value = jnp.maximum(value, jnp.max(best_row[name].T, axis=0, keepdims=True))
        best.append(value)
    if last:
        out_ref[...] = homeward(best).reshape(GROUPS, 1, 128)
    else:
        out_ref[...] = jnp.concatenate(best, axis=0)


def score(blocks, pairs, carried, last, name):
    used = {half for pair in pairs for half in pair[:2]}
    names = tuple(sorted(used | {half[0] + "0" for half in used if EARLY}))
    shape = ((GROUPS, 1, 128) if last else (8, PART), jnp.float32)
    shapes = [shape]
    if pairs is FIRST:
        shapes += [(blocks[half].shape, blocks[half].dtype) for half in KEPT]
    operands = [blocks[half] for half in names + ("ranks",)] + ([] if carried is None else [carried])
    return call(
        functools.partial(score_kernel, names, pairs, last),
        name,
        shapes,
        *operands,
        flops=2 * len(pairs) * PART * PART * D,
    )


FIRST = (
    ("o0", "o0", True, False),
    ("o0", "s0", True, False),
    ("o0", "b0", True, True),
    ("s0", "b0", True, True),
    ("z0", "b0", True, True),
)
SECOND = (
    ("o1", "o1", True, False),
    ("o0", "o1", True, True),
    ("o1", "b0", True, True),
    ("o1", "s1", True, False),
    ("o0", "s1", True, True),
    ("s1", "b0", True, True),
    ("o1", "z0", True, True),
    ("s1", "z0", True, True),
)
THIRD = (
    ("o1", "b1", True, True),
    ("s1", "b1", True, True),
    ("z0", "b1", True, True),
)
FOURTH = (
    ("z1", "b0", True, True),
    ("z1", "b1", True, True),
)


def finish_kernel(own_ref, swap_ref, next_ref, last_ref, pos_ref, out_ref):
    mine = own_ref[...].reshape(GROUPS, 128)
    for index, ref in enumerate((swap_ref, next_ref, last_ref), 1):
        lanes = ref[...].reshape(GROUPS, 128)
        mine = jnp.maximum(mine, pltpu.roll(lanes, 128 - SLOTS * index, 1))
    position = pos_ref[...]
    member = bits(iota((GROUPS, ROWS), 0) == position // SLOTS)
    found = jnp.zeros((SLOTS, ROWS), jnp.float32)
    for part in three_parts(mine[:, :SLOTS]):
        found += dot(part, member, TN)
    here = iota((SLOTS, ROWS), 0) == (position & (SLOTS - 1))
    out_ref[...] = jnp.sum(jnp.where(here, found, 0.0), axis=0, keepdims=True)


FROM_NEXT = [
    (((x + 1) % 4) * 2 + (c if x < 2 else 1 - c), x * 2 + c) for x in range(4) for c in range(2)
]
FROM_LAST = [(((x - 1) % 4) * 2 + c, x * 2 + c) for x in range(4) for c in range(2)]
SWAP = [(x * 2 + 1 - c, x * 2 + c) for x in range(4) for c in range(2)]


def back(pairs):
    return [(there, here) for here, there in pairs]


def send(array, pairs):
    return lax.ppermute(array, ("x", "c"), pairs)


def spread(array):
    return send(array, SWAP), send(array, FROM_NEXT), send(array, FROM_LAST)


def to_home(array):
    return lax.all_to_all(array, ("y", "z"), split_axis=0, concat_axis=0, tiled=True)


def on_device(embeddings, cluster_ids, ranks):
    bf16 = jnp.bfloat16
    first, position = call(
        pack_first,
        "pack_first",
        [((GROUPS, D // 8 + EARLY * HALF, 128), bf16), ((1, ROWS), jnp.int32)],
        embeddings,
        cluster_ids.reshape(1, ROWS),
        flops=2 * PART * ROWS * D,
        scratch=[
            pltpu.VMEM((ROWS, D), jnp.float32),
            pltpu.VMEM((1, ROWS), jnp.int32),
            pltpu.VMEM((ROWS, D), bf16),
            pltpu.SemaphoreType.DMA((CUTS + 1,)),
        ],
        limit=60 * 1024 * 1024,
    )
    table = call(
        pack_table,
        "pack_table",
        [((GROUPS, HALF, 128), bf16)],
        position,
        ranks.reshape(1, ROWS),
    )
    second = call(
        pack_second,
        "pack_second",
        [((GROUPS, D // 8 + (1 - EARLY) * HALF, 128), bf16)],
        embeddings,
        position,
        table,
        *spread(table),
        flops=2 * PART * ROWS * D,
    )
    blocks = {}
    home = to_home(first)
    for half in "01":
        if half == "1":
            home, blocks["ranks"] = call(
                cut_kernel,
                "cut",
                [((GROUPS, D // 8 - EARLY * HALF, 128), bf16), ((GROUPS, HALF, 128), bf16)],
                to_home(second),
            )
        blocks["o" + half] = home
        for block, moved in zip("sbz", spread(home)):
            blocks[block + half] = moved
    best, *kept = score(blocks, FIRST, None, False, "score_first")
    blocks.update(zip(KEPT, kept))
    best = score(blocks, SECOND, best, False, "score_second")
    best = score(blocks, THIRD, best, False, "score_third")
    own = to_home(score(blocks, FOURTH, best, True, "score_fourth"))
    nearest = call(
        finish_kernel,
        "finish",
        [((1, ROWS), jnp.float32)],
        own,
        send(own, back(SWAP)),
        send(own, back(FROM_NEXT)),
        send(own, back(FROM_LAST)),
        position,
    )
    return nearest.reshape(ROWS)


def solution(mesh):
    fine = Mesh(mesh.devices.reshape(tuple(SIZE.values())), tuple(SIZE))
    rows = P(tuple(SIZE))
    return jax.shard_map(
        on_device,
        mesh=fine,
        in_specs=(P(tuple(SIZE), None), P(tuple(SIZE), None), rows),
        out_specs=rows,
        check_vma=False,
    )
```

```python
import functools

import jax
import jax.numpy as jnp
from jax import lax
from jax.experimental import pallas as pl
from jax.experimental.pallas import tpu as pltpu
from jax.sharding import Mesh, PartitionSpec as P

D = 768
ROWS = 512
GROUPS = 32
HALF = 16
SLOTS = 2 * HALF
PART = GROUPS * HALF
PARTS = D // 128
SIZE = {"x": 4, "y": 4, "c": 2, "z": 8}
EARLY = 1
CUTS = 2
LIMIT = 24 * 1024 * 1024
NT = (((1,), (1,)), ((), ()))
NN = (((1,), (0,)), ((), ()))
TN = (((0,), (0,)), ((), ()))
BLOCKS = ("o", "s", "b", "z")
KEPT = ("b0", "z0")
FINALS = tuple(block + half for block in BLOCKS for half in "01")


def dot(a, b, dims):
    return lax.dot_general(a, b, dims, preferred_element_type=jnp.float32)


def iota(shape, axis):
    return lax.broadcasted_iota(jnp.int32, shape, axis)


def bits(mask):
    return mask.astype(jnp.float32).astype(jnp.bfloat16)


def three_parts(value):
    parts = []
    for _ in range(3):
        part = value.astype(jnp.bfloat16)
        parts.append(part)
        value = value - part.astype(jnp.float32)
    return parts


def chosen_rows(position, half):
    slot, group = position & (SLOTS - 1), position // SLOTS
    row = jnp.where(slot // HALF == half, group * HALF + slot % HALF, -1)
    return bits(iota((PART, ROWS), 0) == row)


def put(moved, out_ref, start):
    moved = moved.astype(jnp.bfloat16)
    for part in range(moved.shape[1] // 128):
        rows = start + part * HALF
        out_ref[:, rows : rows + HALF, :] = moved[:, part * 128 : (part + 1) * 128].reshape(
            GROUPS, HALF, 128
        )


def normalise(rows):
    norms = jnp.sum(rows * rows, axis=1, keepdims=True)
    return (rows * lax.rsqrt(norms + 1e-06)).astype(jnp.bfloat16)


def pack_first(emb_hbm, ids_hbm, out_ref, pos_ref, emb_ref, ids_ref, unit_ref, sems):
    pieces = [pl.ds(start, ROWS // CUTS) for start in range(0, ROWS, ROWS // CUTS)]
    small = pltpu.make_async_copy(ids_hbm, ids_ref, sems.at[CUTS])
    copies = [
        pltpu.make_async_copy(emb_hbm.at[piece], emb_ref.at[piece], sems.at[index])
        for index, piece in enumerate(pieces)
    ]
    for copy in [small, *copies]:
        copy.start()
    small.wait()

    target = ids_ref[...]
    member = (iota((GROUPS, ROWS), 0) == target).astype(jnp.float32)
    earlier = bits(iota((ROWS, ROWS), 0) < iota((ROWS, ROWS), 1))
    before = dot(member.astype(jnp.bfloat16), earlier, NN)
    slot = jnp.sum(before * member, axis=0, keepdims=True).astype(jnp.int32)
    position = target * SLOTS + slot
    pos_ref[...] = position

    first, second = chosen_rows(position, 0), chosen_rows(position, 1)
    for copy, piece in zip(copies, pieces):
        copy.wait()
        unit_ref[piece, :] = normalise(emb_ref[piece, :])
    unit = unit_ref[...]
    put(dot(first, unit, NN), out_ref, 0)
    if EARLY:
        put(dot(second, unit[:, : EARLY * 128], NN), out_ref, D // 8)


def pack_table(pos_ref, rank_ref, table_ref):
    rank = rank_ref[...]
    line = iota((128, ROWS), 0)
    ranks = jnp.zeros((PART, 128), jnp.float32)
    for half in range(2):
        parts = jnp.zeros((128, ROWS), jnp.int32)
        for index, part in enumerate(((rank >> 14) - 128, (rank >> 7) & 127, rank & 127)):
            parts = jnp.where(line == 3 * half + index, part, parts)
        chosen = chosen_rows(pos_ref[...], half)
        ranks += dot(chosen, parts.astype(jnp.float32).astype(jnp.bfloat16), NT)
    put(ranks, table_ref, 0)


def pack_second(emb_ref, pos_ref, *refs):
    out_ref = refs[-1]
    unit = normalise(emb_ref[...])
    put(dot(chosen_rows(pos_ref[...], 1), unit[:, EARLY * 128 :], NN), out_ref, 0)
    ranks = jnp.zeros((PART, 128), jnp.float32)
    lane, other = iota((128, 128), 0), iota((128, 128), 1)
    for index, table_ref in enumerate(refs[:-1]):
        moved = bits((lane < 6) & (other == lane + 6 * index))
        ranks += dot(tile(table_ref, 0), moved, NN)
    put(ranks, out_ref, D // 8 - EARLY * HALF)


def vmem(count):
    return [pl.BlockSpec(memory_space=pltpu.VMEM)] * count


def call(kernel, name, shapes, *operands, flops=0, scratch=None, limit=LIMIT):
    shapes = tuple(jax.ShapeDtypeStruct(shape, dtype) for shape, dtype in shapes)
    out = pl.pallas_call(
        kernel,
        out_shape=shapes,
        in_specs=[pl.BlockSpec(memory_space=pltpu.HBM)] * len(operands) if scratch else vmem(len(operands)),
        out_specs=tuple(vmem(len(shapes))),
        scratch_shapes=scratch or [],
        compiler_params=pltpu.CompilerParams(vmem_limit_bytes=limit),
        cost_estimate=pl.CostEstimate(
            flops=flops,
            bytes_accessed=sum(array.size * array.dtype.itemsize for array in operands),
            transcendentals=0,
        ),
        name=name,
    )(*operands)
    return out[0] if len(shapes) == 1 else out


def tile(ref, index):
    return ref[:, index * HALF : (index + 1) * HALF, :].reshape(PART, 128)


def keys_of(data, name):
    if name[1] == "0":
        wide = [tile(data[name], part) for part in range(PARTS)]
    else:
        wide = [tile(data[name[0] + "0"], PARTS + part) for part in range(EARLY)]
        wide += [tile(data[name], part) for part in range(PARTS - EARLY)]
    return jnp.concatenate(wide, axis=1)


def rank_weights(shape, axis, start):
    place = iota(shape, axis) - start
    weights = jnp.where(place == 0, 16384.0, jnp.where(place == 1, 128.0, 1.0))
    return jnp.where((place >= 0) & (place < 3), weights, 0.0).astype(jnp.bfloat16)


def cut_kernel(home_ref, body_ref, ranks_ref):
    body_ref[...] = home_ref[:, : D // 8 - EARLY * HALF, :]
    ranks_ref[...] = home_ref[:, D // 8 - EARLY * HALF :, :]


def homeward(best):
    wide = jnp.concatenate([jnp.broadcast_to(row, (HALF, PART)) for row in best], axis=0)
    own_slot = iota((128, PART), 0) % HALF == iota((128, PART), 1) % HALF
    gather = bits(iota((GROUPS, PART), 1) // HALF == iota((GROUPS, PART), 0))
    total = jnp.zeros((GROUPS, 128), jnp.float32)
    for part in three_parts(jnp.where(own_slot, wide, 0.0)):
        total += dot(gather, part, NT)
    return total


def score_kernel(names, pairs, last, *refs):
    data = dict(zip(names, refs))
    ranks = tile(refs[len(names)], 0)
    refs = refs[len(names) + 1 :]
    if pairs is FIRST:
        carried, (out_ref, *kept) = None, refs
        for name, ref in zip(KEPT, kept):
            ref[...] = data[name][...]
    else:
        carried, out_ref = refs
    used = sorted({name for pair in pairs for name in pair[:2]})
    keys = {name: keys_of(data, name) for name in used}
    by_row, by_lane = {}, {}
    for name in used:
        start = 3 * FINALS.index(name)
        by_row[name] = dot(ranks, rank_weights((128, 128), 0, start), NN)
        by_lane[name] = dot(rank_weights((8, 128), 1, start), ranks, NT)[0:1]
    best_row, best_lane = {}, {}
    for rows, columns, forward, backward in pairs:
        scores = dot(keys[rows], keys[columns], NT)
        row_rank = jnp.concatenate([by_row[rows]] * 4, axis=1)
        lane_rank = by_lane[columns]
        if forward:
            kept = jnp.where(lane_rank < row_rank, scores, -1.0)
            folded = functools.reduce(
                jnp.maximum, [kept[:, 128 * i : 128 * (i + 1)] for i in range(4)]
            )
            best_row[rows] = jnp.maximum(best_row[rows], folded) if rows in best_row else folded
        if backward:
            kept = jnp.where(row_rank < lane_rank, scores, -1.0)
            folded = jnp.max(kept, axis=0, keepdims=True)
            if columns in best_lane:
                folded = jnp.maximum(best_lane[columns], folded)
            best_lane[columns] = folded
    best = []
    for index, name in enumerate(FINALS):
        value = jnp.full((1, PART), -1.0) if carried is None else carried[index : index + 1, :]
        if name in best_lane:
            value = jnp.maximum(value, best_lane[name])
        if name in best_row:
            value = jnp.maximum(value, jnp.max(best_row[name].T, axis=0, keepdims=True))
        best.append(value)
    if last:
        out_ref[...] = homeward(best).reshape(GROUPS, 1, 128)
    else:
        out_ref[...] = jnp.concatenate(best, axis=0)


def score(blocks, pairs, carried, last, name):
    used = {half for pair in pairs for half in pair[:2]}
    names = tuple(sorted(used | {half[0] + "0" for half in used if EARLY}))
    shape = ((GROUPS, 1, 128) if last else (8, PART), jnp.float32)
    shapes = [shape]
    if pairs is FIRST:
        shapes += [(blocks[half].shape, blocks[half].dtype) for half in KEPT]
    operands = [blocks[half] for half in names + ("ranks",)] + ([] if carried is None else [carried])
    return call(
        functools.partial(score_kernel, names, pairs, last),
        name,
        shapes,
        *operands,
        flops=2 * len(pairs) * PART * PART * D,
    )


FIRST = (
    ("o0", "o0", True, False),
    ("o0", "s0", True, False),
    ("o0", "b0", True, True),
    ("s0", "b0", True, True),
    ("z0", "b0", True, True),
)
SECOND = (
    ("o1", "o1", True, False),
    ("o0", "o1", True, True),
    ("o1", "b0", True, True),
    ("o1", "s1", True, False),
    ("o0", "s1", True, True),
    ("s1", "b0", True, True),
    ("o1", "z0", True, True),
    ("s1", "z0", True, True),
)
THIRD = (
    ("o1", "b1", True, True),
    ("s1", "b1", True, True),
    ("z0", "b1", True, True),
)
FOURTH = (
    ("z1", "b0", True, True),
    ("z1", "b1", True, True),
)


def finish_kernel(own_ref, swap_ref, next_ref, last_ref, pos_ref, out_ref):
    mine = own_ref[...].reshape(GROUPS, 128)
    for index, ref in enumerate((swap_ref, next_ref, last_ref), 1):
        lanes = ref[...].reshape(GROUPS, 128)
        mine = jnp.maximum(mine, pltpu.roll(lanes, 128 - SLOTS * index, 1))
    position = pos_ref[...]
    member = bits(iota((GROUPS, ROWS), 0) == position // SLOTS)
    found = jnp.zeros((SLOTS, ROWS), jnp.float32)
    for part in three_parts(mine[:, :SLOTS]):
        found += dot(part, member, TN)
    here = iota((SLOTS, ROWS), 0) == (position & (SLOTS - 1))
    out_ref[...] = jnp.sum(jnp.where(here, found, 0.0), axis=0, keepdims=True)


FROM_NEXT = [
    (((x + 1) % 4) * 2 + (c if x < 2 else 1 - c), x * 2 + c) for x in range(4) for c in range(2)
]
FROM_LAST = [(((x - 1) % 4) * 2 + c, x * 2 + c) for x in range(4) for c in range(2)]
SWAP = [(x * 2 + 1 - c, x * 2 + c) for x in range(4) for c in range(2)]


def back(pairs):
    return [(there, here) for here, there in pairs]


def send(array, pairs):
    return lax.ppermute(array, ("x", "c"), pairs)


def spread(array):
    return send(array, SWAP), send(array, FROM_NEXT), send(array, FROM_LAST)


def to_home(array):
    return lax.all_to_all(array, ("y", "z"), split_axis=0, concat_axis=0, tiled=True)


def on_device(embeddings, cluster_ids, ranks):
    bf16 = jnp.bfloat16
    first, position = call(
        pack_first,
        "pack_first",
        [((GROUPS, D // 8 + EARLY * HALF, 128), bf16), ((1, ROWS), jnp.int32)],
        embeddings,
        cluster_ids.reshape(1, ROWS),
        flops=2 * PART * ROWS * D,
        scratch=[
            pltpu.VMEM((ROWS, D), jnp.float32),
            pltpu.VMEM((1, ROWS), jnp.int32),
            pltpu.VMEM((ROWS, D), bf16),
            pltpu.SemaphoreType.DMA((CUTS + 1,)),
        ],
        limit=60 * 1024 * 1024,
    )
    table = call(
        pack_table,
        "pack_table",
        [((GROUPS, HALF, 128), bf16)],
        position,
        ranks.reshape(1, ROWS),
    )
    second = call(
        pack_second,
        "pack_second",
        [((GROUPS, D // 8 + (1 - EARLY) * HALF, 128), bf16)],
        embeddings,
        position,
        table,
        *spread(table),
        flops=2 * PART * ROWS * D,
    )
    blocks = {}
    home = to_home(first)
    for half in "01":
        if half == "1":
            home, blocks["ranks"] = call(
                cut_kernel,
                "cut",
                [((GROUPS, D // 8 - EARLY * HALF, 128), bf16), ((GROUPS, HALF, 128), bf16)],
                to_home(second),
            )
        blocks["o" + half] = home
        for block, moved in zip("sbz", spread(home)):
            blocks[block + half] = moved
    best, *kept = score(blocks, FIRST, None, False, "score_first")
    blocks.update(zip(KEPT, kept))
    best = score(blocks, SECOND, best, False, "score_second")
    best = score(blocks, THIRD, best, False, "score_third")
    own = to_home(score(blocks, FOURTH, best, True, "score_fourth"))
    nearest = call(
        finish_kernel,
        "finish",
        [((1, ROWS), jnp.float32)],
        own,
        send(own, back(SWAP)),
        send(own, back(FROM_NEXT)),
        send(own, back(FROM_LAST)),
        position,
    )
    return nearest.reshape(ROWS)


def solution(mesh):
    fine = Mesh(mesh.devices.reshape(tuple(SIZE.values())), tuple(SIZE))
    rows = P(tuple(SIZE))
    return jax.shard_map(
        on_device,
        mesh=fine,
        in_specs=(P(tuple(SIZE), None), P(tuple(SIZE), None), rows),
        out_specs=rows,
        check_vma=False,
    )
```

```python
import functools

import jax
import jax.numpy as jnp
from jax import lax
from jax.experimental import pallas as pl
from jax.experimental.pallas import tpu as pltpu
from jax.sharding import Mesh, PartitionSpec as P

D = 768
ROWS = 512
GROUPS = 32
HALF = 16
SLOTS = 2 * HALF
PART = GROUPS * HALF
PARTS = D // 128
SIZE = {"x": 4, "y": 4, "c": 2, "z": 8}
EARLY = 1
CUTS = 2
LIMIT = 24 * 1024 * 1024
NT = (((1,), (1,)), ((), ()))
NN = (((1,), (0,)), ((), ()))
TN = (((0,), (0,)), ((), ()))
BLOCKS = ("o", "s", "b", "z")
KEPT = ("b0", "z0")
FINALS = tuple(block + half for block in BLOCKS for half in "01")


def dot(a, b, dims):
    return lax.dot_general(a, b, dims, preferred_element_type=jnp.float32)


def iota(shape, axis):
    return lax.broadcasted_iota(jnp.int32, shape, axis)


def bits(mask):
    return mask.astype(jnp.float32).astype(jnp.bfloat16)


def three_parts(value):
    parts = []
    for _ in range(3):
        part = value.astype(jnp.bfloat16)
        parts.append(part)
        value = value - part.astype(jnp.float32)
    return parts


def chosen_rows(position, half):
    slot, group = position & (SLOTS - 1), position // SLOTS
    row = jnp.where(slot // HALF == half, group * HALF + slot % HALF, -1)
    return bits(iota((PART, ROWS), 0) == row)


def put(moved, out_ref, start):
    moved = moved.astype(jnp.bfloat16)
    for part in range(moved.shape[1] // 128):
        rows = start + part * HALF
        out_ref[:, rows : rows + HALF, :] = moved[:, part * 128 : (part + 1) * 128].reshape(
            GROUPS, HALF, 128
        )


def normalise(rows):
    norms = jnp.sum(rows * rows, axis=1, keepdims=True)
    return (rows * lax.rsqrt(norms + 1e-06)).astype(jnp.bfloat16)


def pack_first(emb_hbm, ids_hbm, out_ref, pos_ref, emb_ref, ids_ref, unit_ref, sems):
    pieces = [pl.ds(start, ROWS // CUTS) for start in range(0, ROWS, ROWS // CUTS)]
    small = pltpu.make_async_copy(ids_hbm, ids_ref, sems.at[CUTS])
    copies = [
        pltpu.make_async_copy(emb_hbm.at[piece], emb_ref.at[piece], sems.at[index])
        for index, piece in enumerate(pieces)
    ]
    for copy in [small, *copies]:
        copy.start()
    small.wait()

    target = ids_ref[...]
    member = (iota((GROUPS, ROWS), 0) == target).astype(jnp.float32)
    earlier = bits(iota((ROWS, ROWS), 0) < iota((ROWS, ROWS), 1))
    before = dot(member.astype(jnp.bfloat16), earlier, NN)
    slot = jnp.sum(before * member, axis=0, keepdims=True).astype(jnp.int32)
    position = target * SLOTS + slot
    pos_ref[...] = position

    first, second = chosen_rows(position, 0), chosen_rows(position, 1)
    for copy, piece in zip(copies, pieces):
        copy.wait()
        unit_ref[piece, :] = normalise(emb_ref[piece, :])
    unit = unit_ref[...]
    put(dot(first, unit, NN), out_ref, 0)
    if EARLY:
        put(dot(second, unit[:, : EARLY * 128], NN), out_ref, D // 8)


def pack_table(pos_ref, rank_ref, table_ref):
    rank = rank_ref[...]
    line = iota((128, ROWS), 0)
    ranks = jnp.zeros((PART, 128), jnp.float32)
    for half in range(2):
        parts = jnp.zeros((128, ROWS), jnp.int32)
        for index, part in enumerate(((rank >> 14) - 128, (rank >> 7) & 127, rank & 127)):
            parts = jnp.where(line == 3 * half + index, part, parts)
        chosen = chosen_rows(pos_ref[...], half)
        ranks += dot(chosen, parts.astype(jnp.float32).astype(jnp.bfloat16), NT)
    put(ranks, table_ref, 0)


def pack_second(emb_ref, pos_ref, *refs):
    out_ref = refs[-1]
    unit = normalise(emb_ref[...])
    put(dot(chosen_rows(pos_ref[...], 1), unit[:, EARLY * 128 :], NN), out_ref, 0)
    ranks = jnp.zeros((PART, 128), jnp.float32)
    lane, other = iota((128, 128), 0), iota((128, 128), 1)
    for index, table_ref in enumerate(refs[:-1]):
        moved = bits((lane < 6) & (other == lane + 6 * index))
        ranks += dot(tile(table_ref, 0), moved, NN)
    put(ranks, out_ref, D // 8 - EARLY * HALF)


def vmem(count):
    return [pl.BlockSpec(memory_space=pltpu.VMEM)] * count


def call(kernel, name, shapes, *operands, flops=0, scratch=None, limit=LIMIT):
    shapes = tuple(jax.ShapeDtypeStruct(shape, dtype) for shape, dtype in shapes)
    out = pl.pallas_call(
        kernel,
        out_shape=shapes,
        in_specs=[pl.BlockSpec(memory_space=pltpu.HBM)] * len(operands) if scratch else vmem(len(operands)),
        out_specs=tuple(vmem(len(shapes))),
        scratch_shapes=scratch or [],
        compiler_params=pltpu.CompilerParams(vmem_limit_bytes=limit),
        cost_estimate=pl.CostEstimate(
            flops=flops,
            bytes_accessed=sum(array.size * array.dtype.itemsize for array in operands),
            transcendentals=0,
        ),
        name=name,
    )(*operands)
    return out[0] if len(shapes) == 1 else out


def tile(ref, index):
    return ref[:, index * HALF : (index + 1) * HALF, :].reshape(PART, 128)


def keys_of(data, name):
    if name[1] == "0":
        wide = [tile(data[name], part) for part in range(PARTS)]
    else:
        wide = [tile(data[name[0] + "0"], PARTS + part) for part in range(EARLY)]
        wide += [tile(data[name], part) for part in range(PARTS - EARLY)]
    return jnp.concatenate(wide, axis=1)


def rank_weights(shape, axis, start):
    place = iota(shape, axis) - start
    weights = jnp.where(place == 0, 16384.0, jnp.where(place == 1, 128.0, 1.0))
    return jnp.where((place >= 0) & (place < 3), weights, 0.0).astype(jnp.bfloat16)


def cut_kernel(home_ref, body_ref, ranks_ref):
    body_ref[...] = home_ref[:, : D // 8 - EARLY * HALF, :]
    ranks_ref[...] = home_ref[:, D // 8 - EARLY * HALF :, :]


def homeward(best):
    wide = jnp.concatenate([jnp.broadcast_to(row, (HALF, PART)) for row in best], axis=0)
    own_slot = iota((128, PART), 0) % HALF == iota((128, PART), 1) % HALF
    gather = bits(iota((GROUPS, PART), 1) // HALF == iota((GROUPS, PART), 0))
    total = jnp.zeros((GROUPS, 128), jnp.float32)
    for part in three_parts(jnp.where(own_slot, wide, 0.0)):
        total += dot(gather, part, NT)
    return total


def score_kernel(names, pairs, last, *refs):
    data = dict(zip(names, refs))
    ranks = tile(refs[len(names)], 0)
    refs = refs[len(names) + 1 :]
    if pairs is FIRST:
        carried, (out_ref, *kept) = None, refs
        for name, ref in zip(KEPT, kept):
            ref[...] = data[name][...]
    else:
        carried, out_ref = refs
    used = sorted({name for pair in pairs for name in pair[:2]})
    keys = {name: keys_of(data, name) for name in used}
    by_row, by_lane = {}, {}
    for name in used:
        start = 3 * FINALS.index(name)
        by_row[name] = dot(ranks, rank_weights((128, 128), 0, start), NN)
        by_lane[name] = dot(rank_weights((8, 128), 1, start), ranks, NT)[0:1]
    best_row, best_lane = {}, {}
    for rows, columns, forward, backward in pairs:
        scores = dot(keys[rows], keys[columns], NT)
        row_rank = jnp.concatenate([by_row[rows]] * 4, axis=1)
        lane_rank = by_lane[columns]
        if forward:
            kept = jnp.where(lane_rank < row_rank, scores, -1.0)
            folded = functools.reduce(
                jnp.maximum, [kept[:, 128 * i : 128 * (i + 1)] for i in range(4)]
            )
            best_row[rows] = jnp.maximum(best_row[rows], folded) if rows in best_row else folded
        if backward:
            kept = jnp.where(row_rank < lane_rank, scores, -1.0)
            folded = jnp.max(kept, axis=0, keepdims=True)
            if columns in best_lane:
                folded = jnp.maximum(best_lane[columns], folded)
            best_lane[columns] = folded
    best = []
    for index, name in enumerate(FINALS):
        value = jnp.full((1, PART), -1.0) if carried is None else carried[index : index + 1, :]
        if name in best_lane:
            value = jnp.maximum(value, best_lane[name])
        if name in best_row:
            value = jnp.maximum(value, jnp.max(best_row[name].T, axis=0, keepdims=True))
        best.append(value)
    if last:
        out_ref[...] = homeward(best).reshape(GROUPS, 1, 128)
    else:
        out_ref[...] = jnp.concatenate(best, axis=0)


def score(blocks, pairs, carried, last, name):
    used = {half for pair in pairs for half in pair[:2]}
    names = tuple(sorted(used | {half[0] + "0" for half in used if EARLY}))
    shape = ((GROUPS, 1, 128) if last else (8, PART), jnp.float32)
    shapes = [shape]
    if pairs is FIRST:
        shapes += [(blocks[half].shape, blocks[half].dtype) for half in KEPT]
    operands = [blocks[half] for half in names + ("ranks",)] + ([] if carried is None else [carried])
    return call(
        functools.partial(score_kernel, names, pairs, last),
        name,
        shapes,
        *operands,
        flops=2 * len(pairs) * PART * PART * D,
    )


FIRST = (
    ("o0", "o0", True, False),
    ("o0", "s0", True, False),
    ("o0", "b0", True, True),
    ("s0", "b0", True, True),
    ("z0", "b0", True, True),
)
SECOND = (
    ("o1", "o1", True, False),
    ("o0", "o1", True, True),
    ("o1", "b0", True, True),
    ("o1", "z0", True, True),
)
SWAPPED = (
    ("o1", "s1", True, False),
    ("o0", "s1", True, True),
    ("s1", "b0", True, True),
    ("s1", "z0", True, True),
)
THIRD = (
    ("o1", "b1", True, True),
    ("s1", "b1", True, True),
    ("z0", "b1", True, True),
)
FOURTH = (
    ("z1", "b0", True, True),
    ("z1", "b1", True, True),
)


def finish_kernel(own_ref, swap_ref, next_ref, last_ref, pos_ref, out_ref):
    mine = own_ref[...].reshape(GROUPS, 128)
    for index, ref in enumerate((swap_ref, next_ref, last_ref), 1):
        lanes = ref[...].reshape(GROUPS, 128)
        mine = jnp.maximum(mine, pltpu.roll(lanes, 128 - SLOTS * index, 1))
    position = pos_ref[...]
    member = bits(iota((GROUPS, ROWS), 0) == position // SLOTS)
    found = jnp.zeros((SLOTS, ROWS), jnp.float32)
    for part in three_parts(mine[:, :SLOTS]):
        found += dot(part, member, TN)
    here = iota((SLOTS, ROWS), 0) == (position & (SLOTS - 1))
    out_ref[...] = jnp.sum(jnp.where(here, found, 0.0), axis=0, keepdims=True)


FROM_NEXT = [
    (((x + 1) % 4) * 2 + (c if x < 2 else 1 - c), x * 2 + c) for x in range(4) for c in range(2)
]
FROM_LAST = [(((x - 1) % 4) * 2 + c, x * 2 + c) for x in range(4) for c in range(2)]
SWAP = [(x * 2 + 1 - c, x * 2 + c) for x in range(4) for c in range(2)]


def back(pairs):
    return [(there, here) for here, there in pairs]


def send(array, pairs):
    return lax.ppermute(array, ("x", "c"), pairs)


def spread(array):
    return send(array, SWAP), send(array, FROM_NEXT), send(array, FROM_LAST)


def to_home(array):
    return lax.all_to_all(array, ("y", "z"), split_axis=0, concat_axis=0, tiled=True)


def on_device(embeddings, cluster_ids, ranks):
    bf16 = jnp.bfloat16
    first, position = call(
        pack_first,
        "pack_first",
        [((GROUPS, D // 8 + EARLY * HALF, 128), bf16), ((1, ROWS), jnp.int32)],
        embeddings,
        cluster_ids.reshape(1, ROWS),
        flops=2 * PART * ROWS * D,
        scratch=[
            pltpu.VMEM((ROWS, D), jnp.float32),
            pltpu.VMEM((1, ROWS), jnp.int32),
            pltpu.VMEM((ROWS, D), bf16),
            pltpu.SemaphoreType.DMA((CUTS + 1,)),
        ],
        limit=60 * 1024 * 1024,
    )
    table = call(
        pack_table,
        "pack_table",
        [((GROUPS, HALF, 128), bf16)],
        position,
        ranks.reshape(1, ROWS),
    )
    second = call(
        pack_second,
        "pack_second",
        [((GROUPS, D // 8 + (1 - EARLY) * HALF, 128), bf16)],
        embeddings,
        position,
        table,
        *spread(table),
        flops=2 * PART * ROWS * D,
    )
    blocks = {}
    home = to_home(first)
    for half in "01":
        if half == "1":
            home, blocks["ranks"] = call(
                cut_kernel,
                "cut",
                [((GROUPS, D // 8 - EARLY * HALF, 128), bf16), ((GROUPS, HALF, 128), bf16)],
                to_home(second),
            )
        blocks["o" + half] = home
        for block, moved in zip("sbz", spread(home)):
            blocks[block + half] = moved
    best, *kept = score(blocks, FIRST, None, False, "score_first")
    blocks.update(zip(KEPT, kept))
    best = score(blocks, SECOND, best, False, "score_second")
    best = score(blocks, SWAPPED, best, False, "score_swapped")
    best = score(blocks, THIRD, best, False, "score_third")
    own = to_home(score(blocks, FOURTH, best, True, "score_fourth"))
    nearest = call(
        finish_kernel,
        "finish",
        [((1, ROWS), jnp.float32)],
        own,
        send(own, back(SWAP)),
        send(own, back(FROM_NEXT)),
        send(own, back(FROM_LAST)),
        position,
    )
    return nearest.reshape(ROWS)


def solution(mesh):
    fine = Mesh(mesh.devices.reshape(tuple(SIZE.values())), tuple(SIZE))
    rows = P(tuple(SIZE))
    return jax.shard_map(
        on_device,
        mesh=fine,
        in_specs=(P(tuple(SIZE), None), P(tuple(SIZE), None), rows),
        out_specs=rows,
        check_vma=False,
    )
```
